32 devices in a mesh: row: 4 (over y, core), col: 8 (over z, x).
Axes of the slice: x: 2, y: 2, z: 4, core: 2. Of those that a mesh axis runs over, the one named last changes fastest.
Arguments:
- left: bfloat16 [8, 16, 512, 256], P('row', 'col'), may hold values from -0.11767578 to 0.11767578
- right: bfloat16 [8, 16, 512, 256], P('row', 'col'), may hold values from -6 to 6
- lower_inverse: bfloat16 [2, 512, 512], P(None, 'row'), as said below
- upper_inverse: bfloat16 [2, 512, 512], P(None, None, 'col'), as said below
- ranks: int32 [8, 16], P('row', 'col'), may hold values from 16 to 256, as said below
Outputs:
- right_out: bfloat16 [8, 16, 512, 256], P('row', 'col')
The draws below stay inside these ranges and needn't reach their ends.
Inputs may be any that keep to these rules, and one draw needn't show every extreme that they name: Tile ranks: every row of `ranks` contains at least one entry equal to 256; all entries lie in 4..256. Each lower_inverse[k] is lower triangular with a positive diagonal. Each upper_inverse[k] is upper triangular with a positive diagonal.
All inputs are finite; a program needn't handle non-finite values.
Results may differ from the reference program's by a relative error of at most 0.009.
Values may be sent and summed in bfloat16 or wider, within the bound.
A program may use at most 64 MiB of HBM per device.

```python
import jax
import jax.numpy as jnp
from jax import lax

B = 512
R = 256
TR_DEV = 2
TC_DEV = 2
PANELS = 2
NTR = 8
NTC = 16
N_ROW = 4
N_COL = 8


def triangle_draw(key, lower):
    noise_key, diag_key = jax.random.split(jax.random.fold_in(key, 7))
    noise = jax.random.normal(noise_key, (PANELS, B, B), jnp.float32)
    noise = noise * (0.5 * B ** (-0.5))
    diag = jax.random.uniform(diag_key, (PANELS, B, 1), jnp.float32, 0.8, 1.25)
    index = jnp.arange(B, dtype=jnp.int32)
    eye = index[:, None] == index[None, :]
    if lower:
        below = index[:, None] > index[None, :]
    else:
        below = index[:, None] < index[None, :]
    full = jnp.where(eye[None], diag, jnp.where(below[None], noise, 0.0))
    return full.astype(jnp.bfloat16)


def draw_lower_inverse(key, part):
    return triangle_draw(jax.random.fold_in(key, 11), True)


def draw_upper_inverse(key, part):
    return triangle_draw(jax.random.fold_in(key, 13), False)


def draw_ranks(key, part):
    first, second = jax.random.split(jax.random.fold_in(key, 17))
    values = jax.random.randint(first, (NTR, NTC), R // 16, R + 1, jnp.int32)
    chosen = jax.random.randint(second, (NTR,), 0, NTC, jnp.int32)
    columns = jnp.arange(NTC, dtype=jnp.int32)
    return jnp.where(columns[None, :] == chosen[:, None], R, values).astype(jnp.int32)


def block_scale(key, extent, shards, least, high):
    level, own = 1.0, jax.random.fold_in(key, 6)
    for axis_at, parts in shards:
        heights = jnp.exp(jax.random.uniform(jax.random.fold_in(own, axis_at), (parts,), jnp.float32, least / len(shards), high / len(shards)))
        level = level * jnp.repeat(heights, extent[axis_at] // parts).reshape([-1 if axis == axis_at else 1 for axis in range(len(extent))])
    return level


def gaussian(own_key, shape, scale, most, shards=(), held_as=jnp.bfloat16):
    loudness = block_scale(own_key, shape, shards, -0.22, 0.18) if shards else 1.0
    array = jax.random.normal(own_key, shape, jnp.float32) * scale * loudness
    return jnp.minimum(jnp.maximum(array, -most), most).astype(held_as)


def setup_inputs(seed: int = 0) -> dict:
    key_list = jax.random.split(jax.random.key(seed), 6)
    left = gaussian(key_list[0], (NTR, NTC, B, R), ((R * B) ** -0.3333), 0.11767578, ((0, 4), (1, 8)))
    right = gaussian(key_list[1], (NTR, NTC, B, R), 1.0, 6.0, ((0, 4), (1, 8)))
    lower_inverse = draw_lower_inverse(jax.random.fold_in(key_list[5], 71), 0)
    upper_inverse = draw_upper_inverse(jax.random.fold_in(key_list[5], 71), 0)
    ranks = draw_ranks(jax.random.fold_in(key_list[5], 71), 0)
    return {"left": left, "right": right, "lower_inverse": lower_inverse, "upper_inverse": upper_inverse, "ranks": ranks}


def to_tiles(stored):
    rest = stored.shape[2:]
    grid = stored.reshape((N_ROW, TR_DEV, N_COL, TC_DEV) + rest)
    order = (1, 0, 3, 2) + tuple(range(4, 4 + len(rest)))
    return jnp.transpose(grid, order).reshape((NTR, NTC) + rest)


def from_tiles(tiles):
    rest = tiles.shape[2:]
    grid = tiles.reshape((TR_DEV, N_ROW, TC_DEV, N_COL) + rest)
    order = (1, 0, 3, 2) + tuple(range(4, 4 + len(rest)))
    return jnp.transpose(grid, order).reshape((NTR, NTC) + rest)


def reference(left, right, lower_inverse, upper_inverse, ranks):
    slots = jnp.arange(R, dtype=jnp.int32)
    keep = (slots[None, None, :] < ranks[:, :, None]).astype(jnp.bfloat16)
    left = to_tiles(left * keep[:, :, None, :])
    right = to_tiles(right * keep[:, :, None, :])
    columns = jnp.arange(NTC, dtype=jnp.int32)
    for panel in range(PANELS):
        col_left = left[:, panel]
        col_right = jnp.einsum('bc,ibr->icr', upper_inverse[panel].astype(jnp.float32), right[:, panel].astype(jnp.float32)).astype(jnp.bfloat16)
        row_left = jnp.einsum('cb,jbr->jcr', lower_inverse[panel].astype(jnp.float32), left[panel].astype(jnp.float32)).astype(jnp.bfloat16)
        row_right = right[panel].astype(jnp.float32)

        def one_row(items):
            tile_left, tile_right, own_left, own_right, index = items
            core = jnp.einsum('br,jbs->jrs', own_right.astype(jnp.float32), row_left.astype(jnp.float32))
            intersection = jnp.einsum('jbr,bs->jrs', tile_left.astype(jnp.float32), own_left.astype(jnp.float32))
            mixed = jnp.einsum('jrs,jst->jrt', intersection, core, precision=lax.Precision.HIGHEST).astype(jnp.bfloat16)
            change = jnp.einsum('jbt,jrt->jbr', row_right, mixed.astype(jnp.float32))
            fresh = (tile_right.astype(jnp.float32) - change).astype(jnp.bfloat16)
            trail = (index > panel) & (columns > panel)
            on_panel = (index > panel) & (columns == panel)
            kept = jnp.where(on_panel[:, None, None], own_right[None], tile_right)
            return jnp.where(trail[:, None, None], fresh, kept)

        right = lax.map(one_row, (left, right, col_left, col_right, jnp.arange(NTR, dtype=jnp.int32)))
    return from_tiles(right)
```

```python
import functools

import jax
import jax.numpy as jnp
from jax import lax
from jax.experimental import pallas as pl
from jax.experimental.pallas import tpu as pltpu
from jax.sharding import PartitionSpec as P

CHUNKS = 4
MESH = pl.DeviceIdType.MESH


def matmul(a, b):
    return jnp.dot(a, b, preferred_element_type=jnp.float32)


def matmul_tn(a, b):
    return lax.dot_general(a, b, (((0,), (0,)), ((), ())), preferred_element_type=jnp.float32)


def matmul_nt(a, b):
    return lax.dot_general(a, b, (((1,), (1,)), ((), ())), preferred_element_type=jnp.float32)


def children(index, extent, minor, source):
    x, m = lax.rem(index, minor), lax.div(index, minor)
    found = [((x == source) & (m + 1 < extent // minor), index + minor)]
    if source + 1 < minor:
        found.append(((x >= source) & (x + 1 < minor), index + 1))
    if source > 0:
        found.append(((x <= source) & (x >= 1), index - 1))
    return found


def kernel(
    n_row, n_col, minor_col, ranks, left, right, lower, upper, out,
    ul, col_u, col_y, row_y, row_u, low, up,
    send_sem, recv_sem, inv_send, low_recv, up_recv, fetch_sem, swap_sem,
):
    r, c = lax.axis_index("row"), lax.axis_index("col")
    order, width = left.shape[2], left.shape[3]
    step = order // CHUNKS
    fetch_left = [
        [pltpu.make_async_copy(left.at[a, b], ul.at[a, b], fetch_sem.at[0, a, b]) for b in range(2)]
        for a in range(2)
    ]
    fetch_right = [
        [pltpu.make_async_copy(right.at[a, b], out.at[a, b], fetch_sem.at[1, a, b]) for b in range(2)]
        for a in range(2)
    ]
    every = [(1, 0), (0, 0), (0, 1), (1, 1)]
    for a, b in every:
        fetch_left[a][b].start()
    for a, b in every:
        fetch_right[a][b].start()

    barrier = pltpu.get_barrier_semaphore()

    def greet(needed, **target):
        @pl.when(needed)
        def _():
            pl.semaphore_signal(barrier, inc=1, device_id=target, device_id_type=MESH)

    def count(*needed):
        return sum(flag.astype(jnp.int32) for flag in needed)

    x = lax.rem(c, minor_col)
    greet(r >= 2, row=r - 2)
    greet(r >= 0, row=r + 1 - 2 * lax.rem(r, 2))
    greet(x + 1 < minor_col, col=c + 1)
    greet(x >= 1, col=c - 1)
    greet(c >= minor_col, col=c - minor_col)
    for d in range(1, n_row):
        greet(r < 2, row=lax.rem(r + d, n_row))
    for d in range(1, n_col):
        greet(c < 2, col=lax.rem(c + d, n_col))
    greeted = 1 + count(
        r + 2 < n_row, x + 1 < minor_col, x >= 1, c + minor_col < n_col, r != 0, r != 1, c != 0, c != 1
    )

    own_rows = {"up": upper.shape[1], "low": lower.shape[1]}

    def own_up(k):
        rows = own_rows["up"]
        half = pl.ds(pl.multiple_of(lax.rem(r, 2) * (order // 2), order // 2), order // 2)
        return pltpu.make_async_copy(
            upper.at[k, :, half], up.at[pl.ds(k * rows, rows), half], inv_send.at[0, k]
        )

    def own_low(k):
        rows = own_rows["low"]
        return pltpu.make_async_copy(lower.at[k], low.at[pl.ds(k * rows, rows)], inv_send.at[1, k])

    for k in range(2):

        @pl.when(c == k)
        def _():
            own_up(k).start()

        @pl.when(r == k)
        def _():
            own_low(k).start()

    lanes = lax.broadcasted_iota(jnp.int32, (1, width), 1)

    def keep(a, b):
        return (lanes < ranks[a, b]).astype(jnp.float32).astype(jnp.bfloat16)

    buffers = {"cu": col_u, "cy": col_y, "ru": row_u, "ry": row_y}
    place = {
        (kind, k, t): n
        for n, (kind, k, t) in enumerate(
            (kind, k, t) for kind in ("cu", "cy", "ru", "ry") for k in range(2) for t in range(2)
        )
    }

    def axis_of(item):
        return "col" if item[0][0] == "c" else "row"

    def tree(item):
        if axis_of(item) == "col":
            return children(c, n_col, minor_col, item[1])
        return children(r, n_row, 2, item[1])

    def copy_of(item, chunk, way, target):
        kind, k, t = item
        view = buffers[kind].at[k, t, pl.ds(chunk * step, step)]
        return pltpu.make_async_remote_copy(
            src_ref=view,
            dst_ref=view,
            send_sem=send_sem.at[place[item], chunk, way],
            recv_sem=recv_sem.at[place[item], chunk],
            device_id={axis_of(item): target},
            device_id_type=MESH,
        )

    def wanted(item):
        kind, k, t = item
        if t > 0:
            return True
        return (r if axis_of(item) == "col" else c) > k

    def is_source(item):
        return (c if axis_of(item) == "col" else r) == item[1]

    def is_main(item):
        if axis_of(item) == "col":
            return lax.rem(c, minor_col) == item[1]
        return lax.rem(r, 2) == item[1]

    def forward(item, chunk):
        for way, (needed, target) in enumerate(tree(item)):

            @pl.when(needed)
            def _():
                copy_of(item, chunk, way, target).start()

    def send(item, also=True):
        @pl.when(is_source(item) & wanted(item) & also)
        def _():
            for chunk in range(CHUNKS):
                forward(item, chunk)

    def relay(items, also=True, chunks=range(CHUNKS)):
        for chunk in chunks:
            for item, main in items:
                role = is_main(item) if main else jnp.logical_not(is_main(item))

                @pl.when(jnp.logical_not(is_source(item)) & wanted(item) & role & also)
                def _():
                    copy_of(item, chunk, 0, 0).wait_recv()
                    forward(item, chunk)

    def main(*items, also=True):
        relay([(item, True) for item in items], also)

    def leaf(*items, also=True):
        relay([(item, False) for item in items], also)

    half = order // 2
    mine = pl.ds(pl.multiple_of(lax.rem(r, 2) * half, half), half)

    def swap_halves():
        return pltpu.make_async_remote_copy(
            src_ref=up.at[:, mine],
            dst_ref=up.at[:, mine],
            send_sem=swap_sem.at[0],
            recv_sem=swap_sem.at[1],
            device_id={"row": r + 1 - 2 * lax.rem(r, 2)},
            device_id_type=MESH,
        )

    def up_copy(k, source):
        rows = upper.shape[1]
        return pltpu.make_async_remote_copy(
            src_ref=upper.at[k, :, mine],
            dst_ref=up.at[pl.ds(pl.multiple_of(source * rows, rows), rows), mine],
            send_sem=inv_send.at[0, k],
            recv_sem=up_recv.at[source],
            device_id={"col": k},
            device_id_type=MESH,
        )

    def low_copy(k, source):
        rows = lower.shape[1]
        return pltpu.make_async_remote_copy(
            src_ref=lower.at[k],
            dst_ref=low.at[pl.ds(pl.multiple_of(source * rows, rows), rows)],
            send_sem=inv_send.at[1, k],
            recv_sem=low_recv.at[source],
            device_id={"row": k},
            device_id_type=MESH,
        )

    for a in range(2):
        fetch_left[a][0].wait()
        ul[a, 0] = ul[a, 0] * keep(a, 0)
        for k in range(2):

            @pl.when(c == k)
            def _():
                col_u[k, a] = ul[a, 0]

    pl.semaphore_wait(barrier, greeted)

    for k in range(2):

        @pl.when(c != k)
        def _():
            up_copy(k, c).start()

        @pl.when(r != k)
        def _():
            low_copy(k, r).start()

    send(("cu", 0, 0))
    send(("cu", 0, 1), also=r >= 2)
    send(("cu", 1, 0))
    send(("cu", 1, 1))
    for a, b in ((0, 0), (0, 1), (1, 0), (1, 1)):
        fetch_right[a][b].wait()
        out[a, b] = out[a, b] * keep(a, b)
        if a == 0:

            @pl.when(r == 0)
            def _():
                row_y[0, b] = out[0, b]

            send(("ry", 0, b))
    for a, b in ((0, 1), (1, 1)):
        fetch_left[a][b].wait()
        ul[a, b] = ul[a, b] * keep(a, b)

    for k in range(2):

        @pl.when(c == k)
        def _():
            own_up(k).wait()

        @pl.when(r == k)
        def _():
            own_low(k).wait()

    @pl.when(c < 2)
    def _():
        for s in range(n_col):

            @pl.when(s != c)
            def _():
                up_copy(0, s).wait_recv()

        swap_halves().start()
        swap_halves().wait_recv()

    @pl.when(c == 0)
    def _():
        col_y[0, 0] = matmul(up[...], out[0, 0]).astype(jnp.bfloat16)

    send(("cy", 0, 0))
    send(("cu", 0, 1), also=r < 2)

    @pl.when(c == 0)
    def _():
        col_y[0, 1] = matmul(up[...], out[1, 0]).astype(jnp.bfloat16)

    send(("cy", 0, 1))

    @pl.when(r < 2)
    def _():
        for s in range(n_row):

            @pl.when(s != r)
            def _():
                low_copy(0, s).wait_recv()

    for b in range(2):
        for k in range(2):

            @pl.when(r == k)
            def _():
                row_u[k, b] = matmul(low[...], ul[0, b]).astype(jnp.bfloat16)

            send(("ru", k, b))

    def update(panel, a, b, also=True):
        row_in = (a * n_row + r) > panel
        tile_col = b * n_col + c

        @pl.when(row_in & (tile_col > panel) & also)
        def _():
            core = matmul_tn(col_y[panel, a], row_u[panel, b]).astype(jnp.bfloat16)
            meet = matmul_tn(ul[a, b], col_u[panel, a]).astype(jnp.bfloat16)
            mixed = matmul(meet, core).astype(jnp.bfloat16)
            change = matmul_nt(row_y[panel, b], mixed)
            out[a, b] = (out[a, b].astype(jnp.float32) - change).astype(jnp.bfloat16)

        if b == 0:

            @pl.when(row_in & (c == panel) & also)
            def _():
                out[a, 0] = col_y[panel, a]

    def solve_next(a):
        @pl.when(c == 1)
        def _():
            col_y[1, a] = matmul(up[...], out[a, 0]).astype(jnp.bfloat16)

        send(("cy", 1, a))

    def share_row(b):
        @pl.when(r == 1)
        def _():
            row_y[1, b] = out[0, b]

        send(("ry", 1, b))

    main(("cu", 0, 0), ("cu", 1, 0), ("ry", 0, 0))
    main(("cy", 0, 0), also=r < 2)
    leaf(("cu", 0, 0), ("ry", 0, 0), ("cy", 0, 0), ("ru", 0, 0), also=r == 1)
    update(0, 0, 0, also=r == 1)
    share_row(0)
    leaf(("ry", 0, 1), ("ru", 0, 1), also=r == 1)
    update(0, 0, 1, also=r == 1)
    share_row(1)
    main(("cu", 0, 1), ("cu", 1, 1), ("ry", 0, 1))
    main(("cy", 0, 0), ("ru", 0, 0), also=r >= 2)
    main(("ru", 1, 0))
    leaf(("cu", 0, 0), ("ry", 0, 0), ("cy", 0, 0), ("ru", 0, 0), also=r != 1)
    update(0, 0, 0, also=r != 1)
    solve_next(0)
    main(("cy", 0, 1), ("cy", 1, 0), ("ru", 0, 1), ("ru", 1, 1))
    leaf(("cu", 0, 1))
    leaf(("cy", 0, 1))
    update(0, 1, 0, also=c == 1)
    solve_next(1)
    leaf(("ry", 0, 1), ("ru", 0, 1), also=r != 1)
    quarter = CHUNKS // 4
    last = [range(quarter * n, quarter * (n + 1)) for n in range(4)]
    relay([(("cy", 1, 1), True)], chunks=last[0])
    update(0, 1, 0, also=c != 1)
    relay([(("cy", 1, 1), True)], chunks=last[1])
    update(0, 0, 1, also=r != 1)
    relay([(("cy", 1, 1), True)], chunks=last[2])
    update(0, 1, 1)
    relay([(("cy", 1, 1), True)], chunks=last[3])
    main(("ry", 1, 0))
    main(("ry", 1, 1))
    leaf(("cu", 1, 0), ("cy", 1, 0), ("ru", 1, 0), ("ry", 1, 0))
    update(1, 0, 0)
    leaf(("ru", 1, 1), ("ry", 1, 1), ("cu", 1, 1))
    update(1, 0, 1)
    leaf(("cy", 1, 1))
    update(1, 1, 0)
    update(1, 1, 1)

    for k in range(2):

        @pl.when(c != k)
        def _():
            up_copy(k, c).wait_send()

        @pl.when(r != k)
        def _():
            low_copy(k, r).wait_send()

    @pl.when(c < 2)
    def _():
        swap_halves().wait_send()

    for item in place:
        for way, (needed, target) in enumerate(tree(item)):

            @pl.when(needed & wanted(item))
            def _():
                for chunk in range(CHUNKS):
                    copy_of(item, chunk, way, target).wait_send()


def body(left, right, lower_inverse, upper_inverse, ranks):
    n_row, n_col = lax.axis_size("row"), lax.axis_size("col")
    minor_col = 4 if n_col % 4 == 0 and n_col > 8 else 2
    order, width = left.shape[2:]
    upper = jnp.swapaxes(upper_inverse, 1, 2)
    tile = (order, width)
    vmem = pl.BlockSpec(memory_space=pltpu.VMEM)
    hbm = pl.BlockSpec(memory_space=pltpu.HBM)
    return pl.pallas_call(
        functools.partial(kernel, n_row, n_col, minor_col),
        out_shape=jax.ShapeDtypeStruct(right.shape, jnp.bfloat16),
        in_specs=[pl.BlockSpec(memory_space=pltpu.SMEM)] + [hbm] * 4,
        out_specs=vmem,
        scratch_shapes=[
            pltpu.VMEM((2, 2) + tile, jnp.bfloat16),
            pltpu.VMEM((2, 2) + tile, jnp.bfloat16),
            pltpu.VMEM((2, 2) + tile, jnp.bfloat16),
            pltpu.VMEM((2, 2) + tile, jnp.bfloat16),
            pltpu.VMEM((2, 2) + tile, jnp.bfloat16),
            pltpu.VMEM((order, order), jnp.bfloat16),
            pltpu.VMEM((order, order), jnp.bfloat16),
            pltpu.SemaphoreType.DMA((16, CHUNKS, 3)),
            pltpu.SemaphoreType.DMA((16, CHUNKS)),
            pltpu.SemaphoreType.DMA((2, 2)),
            pltpu.SemaphoreType.DMA((n_row,)),
            pltpu.SemaphoreType.DMA((n_col,)),
            pltpu.SemaphoreType.DMA((2, 2, 2)),
            pltpu.SemaphoreType.DMA((2,)),
        ],
        compiler_params=pltpu.CompilerParams(
            collective_id=0, has_side_effects=True, vmem_limit_bytes=60 * 1024 * 1024
        ),
        cost_estimate=pl.CostEstimate(
            flops=2_000_000_000, bytes_accessed=4_000_000, transcendentals=0
        ),
    )(ranks, left, right, lower_inverse, upper)


def solution(mesh):
    placed = (
        P("row", "col", None, None),
        P("row", "col", None, None),
        P(None, "row", None),
        P(None, None, "col"),
        P("row", "col"),
    )
    return jax.shard_map(
        body, mesh=mesh, in_specs=placed, out_specs=P("row", "col", None, None), check_vma=False
    )
```

```python
import functools

import jax
import jax.numpy as jnp
from jax import lax
from jax.experimental import pallas as pl
from jax.experimental.pallas import tpu as pltpu
from jax.sharding import PartitionSpec as P

CHUNKS = 8
MESH = pl.DeviceIdType.MESH


def matmul(a, b):
    return jnp.dot(a, b, preferred_element_type=jnp.float32)


def matmul_tn(a, b):
    return lax.dot_general(a, b, (((0,), (0,)), ((), ())), preferred_element_type=jnp.float32)


def matmul_nt(a, b):
    return lax.dot_general(a, b, (((1,), (1,)), ((), ())), preferred_element_type=jnp.float32)


def kernel(
    n_row, n_col, minor_col, ranks, left, right, lower, upper, out,
    ul, colb, rowb, low, up, mix,
    col_send, col_recv, row_send, row_recv, inv_send, low_recv, up_recv, fetch_sem, swap_sem, extra_sem,
):
    r, c = lax.axis_index("row"), lax.axis_index("col")
    x, core = lax.rem(c, minor_col), lax.rem(r, 2)
    order, width = left.shape[2], left.shape[3]
    step = order // CHUNKS
    fetch_left = [
        [pltpu.make_async_copy(left.at[a, b], ul.at[a, b], fetch_sem.at[0, a, b]) for b in range(2)]
        for a in range(2)
    ]
    fetch_right = [
        [pltpu.make_async_copy(right.at[a, b], out.at[a, b], fetch_sem.at[1, a, b]) for b in range(2)]
        for a in range(2)
    ]
    every = [(0, 0), (1, 0), (0, 1), (1, 1)]
    for a, b in every:
        fetch_left[a][b].start()
    for a, b in every:
        fetch_right[a][b].start()

    barrier = pltpu.get_barrier_semaphore()

    def greet(needed, **target):
        @pl.when(needed)
        def _():
            pl.semaphore_signal(barrier, inc=1, device_id=target, device_id_type=MESH)

    def count(*needed):
        return sum(flag.astype(jnp.int32) for flag in needed)

    greet(c >= minor_col, col=c - minor_col)
    greet(r >= 2, row=r - 2)
    greet(r >= 0, row=r + 1 - 2 * core)
    greet(x + 1 < minor_col, col=c + 1)
    greet(x >= 1, col=c - 1)
    for d in range(1, n_row):
        greet(r < 2, row=lax.rem(r + d, n_row))
    for d in range(1, n_col):
        greet(c < 2, col=lax.rem(c + d, n_col))
    greeted = 1 + count(
        r + 2 < n_row, x + 1 < minor_col, x >= 1, c + minor_col < n_col, r != 0, r != 1, c != 0, c != 1
    )

    half = order // 2
    mine = pl.ds(pl.multiple_of(core * half, half), half)
    up_rows, low_rows = upper.shape[1], lower.shape[1]

    def own_up(k):
        return pltpu.make_async_copy(
            upper.at[k, :, mine], up.at[pl.ds(k * up_rows, up_rows), mine], inv_send.at[0, k]
        )

    def own_low(k):
        return pltpu.make_async_copy(
            lower.at[k], low.at[pl.ds(k * low_rows, low_rows)], inv_send.at[1, k]
        )

    for k in range(2):

        @pl.when(c == k)
        def _():
            own_up(k).start()

        @pl.when(r == k)
        def _():
            own_low(k).start()

    lanes = lax.broadcasted_iota(jnp.int32, (1, width), 1)

    def keep(a, b):
        return (lanes < ranks[a, b]).astype(jnp.float32).astype(jnp.bfloat16)

    def col_slot(kind, k, t):
        return 2 * t + kind if k == 0 else 2 * kind + t

    def row_slot(kind, k, t):
        return 2 * (1 - kind) + t if k == 0 else 2 * kind + t

    def col_wanted(k, slot):
        t = slot // 2 if k == 0 else slot % 2
        return True if t > 0 else r > k

    def row_wanted(k, slot):
        return True if slot % 2 > 0 or (k, slot) == (0, 2) else c > k

    def piece(q):
        return pl.ds(pl.multiple_of(q * step, step), step)

    def col_copy(k, slot, q, way, target):
        view = colb.at[k, slot] if q is None else colb.at[k, slot, piece(q)]
        return pltpu.make_async_remote_copy(
            src_ref=view,
            dst_ref=view,
            send_sem=col_send.at[k, slot, way],
            recv_sem=col_recv.at[k, slot, 0 if q is None else q],
            device_id={"col": target},
            device_id_type=MESH,
        )

    def row_copy(k, slot, q, way, target):
        view = rowb.at[k, slot] if q is None else rowb.at[k, slot, piece(q)]
        return pltpu.make_async_remote_copy(
            src_ref=view,
            dst_ref=view,
            send_sem=row_send.at[k, slot, way],
            recv_sem=row_recv.at[k, slot, 0 if q is None else q],
            device_id={"row": target},
            device_id_type=MESH,
        )

    def col_ways(k):
        return [
            ((x == k) & (c + minor_col < n_col), c + minor_col),
            ((x >= k) & (x + 1 < minor_col), c + 1),
            ((x <= k) & (x >= 1), c - 1),
        ]

    def row_ways():
        return [(r + 2 < n_row, r + 2), (r >= 0, r + 1 - 2 * core)]

    def col_forward(k, slot, q, ways=(0, 1, 2)):
        for way in ways:
            needed, target = col_ways(k)[way]

            @pl.when(needed)
            def _():
                col_copy(k, slot, q, way, target).start()

    def row_forward(k, slot, q):
        for way, (needed, target) in enumerate(row_ways()):

            @pl.when(needed)
            def _():
                row_copy(k, slot, q, way, target).start()

    def col_send_out(k, slot, ways=(0, 1, 2)):
        @pl.when((c == k) & col_wanted(k, slot))
        def _():
            @pl.loop(0, CHUNKS)
            def _(q):
                col_forward(k, slot, q, ways)

    def row_send_out(k, slot):
        @pl.when((r == k) & row_wanted(k, slot))
        def _():
            @pl.loop(0, CHUNKS)
            def _(q):
                row_forward(k, slot, q)

    trunk = jnp.minimum(x, 1)

    def col_relay_piece(slot, q):
        col_copy(trunk, slot, q, 0, 0).wait_recv()
        col_forward(trunk, slot, q)

    def col_relay(slot, also):
        @pl.when((c >= 2) & (x < 2) & also)
        def _():
            @pl.loop(0, CHUNKS)
            def _(q):
                col_relay_piece(slot, q)

    def row_relay_piece(slot, q):
        row_copy(core, slot, q, 0, 0).wait_recv()
        row_forward(core, slot, q)

    def row_relay(slot, also):
        @pl.when((r >= 2) & also)
        def _():
            @pl.loop(0, CHUNKS)
            def _(q):
                row_relay_piece(slot, q)

    def col_leaf(k, *slots, also=True):
        for slot in slots:

            @pl.when((x != k) & col_wanted(k, slot) & also)
            def _():
                @pl.loop(0, CHUNKS)
                def _(q):
                    col_copy(k, slot, q, 0, 0).wait_recv()
                    if minor_col > 2:
                        col_forward(k, slot, q, (1, 2))

    def row_leaf(k, *slots, also=True):
        for slot in slots:

            @pl.when((core != k) & row_wanted(k, slot) & also)
            def _():
                @pl.loop(0, CHUNKS)
                def _(q):
                    row_copy(k, slot, q, 0, 0).wait_recv()

    def swap_halves():
        return pltpu.make_async_remote_copy(
            src_ref=up.at[:, mine],
            dst_ref=up.at[:, mine],
            send_sem=swap_sem.at[0],
            recv_sem=swap_sem.at[1],
            device_id={"row": r + 1 - 2 * core},
            device_id_type=MESH,
        )

    def up_copy(k, source):
        return pltpu.make_async_remote_copy(
            src_ref=upper.at[k, :, mine],
            dst_ref=up.at[pl.ds(pl.multiple_of(source * up_rows, up_rows), up_rows), mine],
            send_sem=inv_send.at[0, k],
            recv_sem=up_recv.at[source],
            device_id={"col": k},
            device_id_type=MESH,
        )

    def low_copy(k, source):
        return pltpu.make_async_remote_copy(
            src_ref=lower.at[k],
            dst_ref=low.at[pl.ds(pl.multiple_of(source * low_rows, low_rows), low_rows)],
            send_sem=inv_send.at[1, k],
            recv_sem=low_recv.at[source],
            device_id={"row": k},
            device_id_type=MESH,
        )

    def lend_left():
        return pltpu.make_async_remote_copy(
            src_ref=ul.at[0, 0],
            dst_ref=colb.at[0, 0],
            send_sem=extra_sem.at[0],
            recv_sem=extra_sem.at[1],
            device_id={"col": 0},
            device_id_type=MESH,
        )

    def pass_mixed():
        return pltpu.make_async_remote_copy(
            src_ref=mix,
            dst_ref=mix,
            send_sem=extra_sem.at[2],
            recv_sem=extra_sem.at[3],
            device_id={"col": 1},
            device_id_type=MESH,
        )

    U, Y = 0, 1

    for a, b in every:
        fetch_left[a][b].wait()
        ul[a, b] = ul[a, b] * keep(a, b)
        if b == 0:
            for k in range(2):
                slot = col_slot(U, k, a)

                @pl.when((c == k) & col_wanted(k, slot))
                def _():
                    colb[k, slot] = ul[a, 0]

    for a, b in every:
        fetch_right[a][b].wait()
        out[a, b] = out[a, b] * keep(a, b)
        if a == 0:

            @pl.when(r == 0)
            def _():
                rowb[0, row_slot(Y, 0, b)] = out[0, b]

    pl.semaphore_wait(barrier, greeted)

    for k in range(2):

        @pl.when(c != k)
        def _():
            up_copy(k, c).start()

        @pl.when(r != k)
        def _():
            low_copy(k, r).start()

    def core_of(panel, a, b):
        return matmul_tn(
            colb[panel, col_slot(Y, panel, a)], rowb[panel, row_slot(U, panel, b)]
        ).astype(jnp.bfloat16)

    def subtract(panel, a, b, mixed):
        change = matmul_nt(rowb[panel, row_slot(Y, panel, b)], mixed)
        out[a, b] = (out[a, b].astype(jnp.float32) - change).astype(jnp.bfloat16)

    def update(panel, a, b, also=True):
        @pl.when((True if a > 0 else r > panel) & also)
        def _():
            meet = matmul_tn(ul[a, b], colb[panel, col_slot(U, panel, a)]).astype(jnp.bfloat16)
            mixed = matmul(meet, core_of(panel, a, b)).astype(jnp.bfloat16)
            subtract(panel, a, b, mixed)

    def wait_low(k):
        own_low(k).wait()
        for s in range(n_row):
            if s != k:
                low_copy(k, s).wait_recv()

    def solve_row(k, b, source=None):
        slot = row_slot(U, k, b)
        rowb[k, slot] = matmul(low[...], ul[0, b] if source is None else source[...]).astype(jnp.bfloat16)

    def solve_col(k, a):
        colb[k, col_slot(Y, k, a)] = matmul(up[...], out[a, 0]).astype(jnp.bfloat16)

    def share_row(b):
        rowb[1, row_slot(Y, 1, b)] = out[0, b]
        row_send_out(1, row_slot(Y, 1, b))

    even, odd = (r >= 2) & (core == 0), (r >= 2) & (core == 1)

    @pl.when(r == 0)
    def _():
        row_send_out(0, 0)
        row_send_out(0, 1)

    @pl.when(c < 2)
    def _():
        @pl.when((c == 1) & (r == 0))
        def _():
            lend_left().start()

        col_send_out(0, 0)
        col_send_out(1, 1, (1, 2))
        col_send_out(1, 0, (0,))
        col_send_out(1, 1, (0,))
        col_send_out(1, 0, (1, 2))

        @pl.when(r == 0)
        def _():
            wait_low(0)

            @pl.when(c == 0)
            def _():
                lend_left().wait_recv()
                solve_row(0, 0, colb.at[0, 0])

            @pl.when(c != 0)
            def _():
                solve_row(0, 0)

            row_send_out(0, 2)
            solve_row(0, 1)
            row_send_out(0, 3)

        for k in range(2):

            @pl.when(c == k)
            def _():
                own_up(k).wait()

        for s in range(n_col):

            @pl.when(s != c)
            def _():
                up_copy(0, s).wait_recv()

        swap_halves().start()
        swap_halves().wait_recv()

        @pl.when(c == 0)
        def _():
            @pl.when(r > 0)
            def _():
                solve_col(0, 0)

            col_send_out(0, 1)
            col_send_out(0, 2, (0,))
            solve_col(0, 1)
            col_send_out(0, 3, (0,))

        @pl.when(r == 1)
        def _():
            wait_low(1)
            solve_row(1, 1)
            row_send_out(1, 1)

        row_relay(0, even & (c == 1))
        row_relay(1, even)
        row_relay(2, even)
        row_leaf(0, 0, 2)

        @pl.when(c == 0)
        def _():
            col_leaf(1, 1)
            meet = matmul_tn(colb[1, col_slot(U, 1, 1)], ul[1, 0]).astype(jnp.bfloat16)
            mix[...] = matmul(meet, core_of(0, 1, 0)).astype(jnp.bfloat16)
            pass_mixed().start()
            col_send_out(0, 2, (1, 2))
            col_send_out(0, 3, (1, 2))

        @pl.when(c == 1)
        def _():
            col_leaf(0, 0, 1)
            update(0, 0, 0)

            @pl.when(r > 1)
            def _():
                solve_col(1, 0)

            col_send_out(1, 2)

        row_relay(3, even)
        row_leaf(0, 1, 3)
        update(0, 0, 1, also=r == 1)

        @pl.when(r == 1)
        def _():
            share_row(1)

        @pl.when(c == 1)
        def _():
            pass_mixed().wait_recv()
            subtract(0, 1, 0, mix[...])
            solve_col(1, 1)
            col_send_out(1, 3)

        row_relay(1, odd)
        update(0, 0, 1, also=r != 1)
        col_leaf(0, 2, 3)
        update(0, 1, 1)
        row_relay(3, odd)
        row_leaf(1, 1, 3)
        col_leaf(1, 0)
        col_leaf(1, 1, also=c != 0)
        col_leaf(1, 2)
        update(1, 0, 1)
        col_leaf(1, 3)
        update(1, 1, 1)
        for panel in range(2):
            for a in range(2):

                @pl.when((c == panel) & (True if a > 0 else r > panel))
                def _():
                    out[a, 0] = colb[panel, col_slot(Y, panel, a)]

    @pl.when((c >= 2) & (r < 2))
    def _():
        @pl.when(r == 0)
        def _():
            wait_low(0)
            for b in range(2):
                solve_row(0, b)
                row_send_out(0, 2 + b)

        col_relay(0, (r == 1) & (x == 0))
        col_relay(1, x == 1)
        col_relay(2, (r == 0) & (x == 0))

        @pl.when(r == 1)
        def _():
            wait_low(1)
            for b in range(2):
                solve_row(1, b)
                row_send_out(1, b)

            col_relay(1, x == 0)
            col_leaf(0, 0, 1)
            for b in range(2):
                row_leaf(0, b, 2 + b)
                update(0, 0, b)
                share_row(b)

            col_relay(2, x == 0)

        col_relay(3, x == 0)
        col_leaf(0, 2, 3)
        update(0, 1, 0)
        update(0, 1, 1)
        col_relay(3, x == 1)
        col_leaf(1, 1, 3)
        for b in range(2):
            row_leaf(1, b, 2 + b)
            update(1, 1, b)

    @pl.when((c >= 2) & (r >= 2))
    def _():
        main = x < 2

        def pump(slot, even_rows, odd_rows):
            @pl.loop(0, CHUNKS)
            def _(q):
                @pl.when(main)
                def _():
                    col_relay_piece(slot, q)

                for role, rows in ((core == 0, even_rows), (core == 1, odd_rows)):
                    for first, rate in rows:
                        for extra in range(rate):

                            @pl.when(role)
                            def _():
                                m = first * CHUNKS + q * rate + extra
                                row_relay_piece(m // CHUNKS, lax.rem(m, CHUNKS))

        pump(0, [(0, 1)], [])
        pump(1, [(1, 2)], [])
        col_leaf(0, 0, 1)
        row_leaf(0, 0, 2)
        update(0, 0, 0)
        pump(2, [(3, 1)], [(0, 2)])
        row_leaf(0, 1, 3)
        update(0, 0, 1)
        pump(3, [], [(2, 2)])
        col_leaf(1, 0, 2)
        for b in range(2):
            row_leaf(1, b, 2 + b)
            update(1, 0, b)
        col_leaf(0, 2, 3)
        update(0, 1, 0)
        update(0, 1, 1)
        col_leaf(1, 1, 3)
        update(1, 1, 0)
        update(1, 1, 1)

    for k in range(2):

        @pl.when(c != k)
        def _():
            up_copy(k, c).wait_send()

        @pl.when(r != k)
        def _():
            low_copy(k, r).wait_send()

    @pl.when(c < 2)
    def _():
        swap_halves().wait_send()

        @pl.when((c == 1) & (r == 0))
        def _():
            lend_left().wait_send()

        @pl.when(c == 0)
        def _():
            pass_mixed().wait_send()

    for k in range(2):
        for slot in range(4):
            for way, (needed, target) in enumerate(col_ways(k)):

                @pl.when(needed & col_wanted(k, slot))
                def _():
                    col_copy(k, slot, None, way, target).wait_send()

            for way, (needed, target) in enumerate(row_ways()):

                @pl.when((core == k) & needed & row_wanted(k, slot))
                def _():
                    row_copy(k, slot, None, way, target).wait_send()


def body(left, right, lower_inverse, upper_inverse, ranks):
    n_row, n_col = lax.axis_size("row"), lax.axis_size("col")
    minor_col = 4 if n_col % 4 == 0 and n_col > 8 else 2
    order, width = left.shape[2:]
    upper = jnp.swapaxes(upper_inverse, 1, 2)
    tile = (order, width)
    vmem = pl.BlockSpec(memory_space=pltpu.VMEM)
    hbm = pl.BlockSpec(memory_space=pltpu.HBM)
    return pl.pallas_call(
        functools.partial(kernel, n_row, n_col, minor_col),
        out_shape=jax.ShapeDtypeStruct(right.shape, jnp.bfloat16),
        in_specs=[pl.BlockSpec(memory_space=pltpu.SMEM)] + [hbm] * 4,
        out_specs=vmem,
        scratch_shapes=[
            pltpu.VMEM((2, 2) + tile, jnp.bfloat16),
            pltpu.VMEM((2, 4) + tile, jnp.bfloat16),
            pltpu.VMEM((2, 4) + tile, jnp.bfloat16),
            pltpu.VMEM((order, order), jnp.bfloat16),
            pltpu.VMEM((order, order), jnp.bfloat16),
            pltpu.VMEM((width, width), jnp.bfloat16),
            pltpu.SemaphoreType.DMA((2, 4, 3)),
            pltpu.SemaphoreType.DMA((2, 4, CHUNKS)),
            pltpu.SemaphoreType.DMA((2, 4, 2)),
            pltpu.SemaphoreType.DMA((2, 4, CHUNKS)),
            pltpu.SemaphoreType.DMA((2, 2)),
            pltpu.SemaphoreType.DMA((n_row,)),
            pltpu.SemaphoreType.DMA((n_col,)),
            pltpu.SemaphoreType.DMA((2, 2, 2)),
            pltpu.SemaphoreType.DMA((2,)),
            pltpu.SemaphoreType.DMA((4,)),
        ],
        compiler_params=pltpu.CompilerParams(
            collective_id=0, has_side_effects=True, vmem_limit_bytes=60 * 1024 * 1024
        ),
        cost_estimate=pl.CostEstimate(
            flops=2_000_000_000, bytes_accessed=4_000_000, transcendentals=0
        ),
    )(ranks, left, right, lower_inverse, upper)


def solution(mesh):
    placed = (
        P("row", "col", None, None),
        P("row", "col", None, None),
        P(None, "row", None),
        P(None, None, "col"),
        P("row", "col"),
    )
    return jax.shard_map(
        body, mesh=mesh, in_specs=placed, out_specs=P("row", "col", None, None), check_vma=False
    )
```

```python
import functools

import jax
import jax.numpy as jnp
from jax import lax
from jax.experimental import pallas as pl
from jax.experimental.pallas import tpu as pltpu
from jax.sharding import PartitionSpec as P

CHUNKS = 8
MESH = pl.DeviceIdType.MESH


def matmul(a, b):
    return jnp.dot(a, b, preferred_element_type=jnp.float32)


def matmul_tn(a, b):
    return lax.dot_general(a, b, (((0,), (0,)), ((), ())), preferred_element_type=jnp.float32)


def matmul_nt(a, b):
    return lax.dot_general(a, b, (((1,), (1,)), ((), ())), preferred_element_type=jnp.float32)


def kernel(
    n_row, n_col, minor_col, ranks, left, right, lower, upper, out,
    ul, colb, rowb, low, up, mix,
    col_send, col_recv, row_send, row_recv, inv_send, low_recv, up_recv, fetch_sem, swap_sem, extra_sem,
):
    r, c = lax.axis_index("row"), lax.axis_index("col")
    x, core = lax.rem(c, minor_col), lax.rem(r, 2)
    order, width = left.shape[2], left.shape[3]
    step = order // CHUNKS
    fetch_left = [
        [pltpu.make_async_copy(left.at[a, b], ul.at[a, b], fetch_sem.at[0, a, b]) for b in range(2)]
        for a in range(2)
    ]
    fetch_right = [
        [pltpu.make_async_copy(right.at[a, b], out.at[a, b], fetch_sem.at[1, a, b]) for b in range(2)]
        for a in range(2)
    ]
    every = [(0, 0), (1, 0), (0, 1), (1, 1)]
    for a, b in every:
        fetch_left[a][b].start()
    for a, b in every:
        fetch_right[a][b].start()

    @pl.when(c < 2)
    def _():
        up[...] = jnp.zeros_like(up)

    barrier = pltpu.get_barrier_semaphore()

    def greet(needed, **target):
        @pl.when(needed)
        def _():
            pl.semaphore_signal(barrier, inc=1, device_id=target, device_id_type=MESH)

    def count(*needed):
        return sum(flag.astype(jnp.int32) for flag in needed)

    greet(c >= minor_col, col=c - minor_col)
    greet(r >= 2, row=r - 2)
    greet(r >= 0, row=r + 1 - 2 * core)
    greet(x + 1 < minor_col, col=c + 1)
    greet(x >= 1, col=c - 1)
    for d in range(1, n_row):
        greet(r < 2, row=lax.rem(r + d, n_row))
    for d in range(1, n_col):
        greet(c < 2, col=lax.rem(c + d, n_col))
    greeted = 1 + count(
        r + 2 < n_row, x + 1 < minor_col, x >= 1, c + minor_col < n_col, r != 0, r != 1, c != 0, c != 1
    )

    half = order // 2
    mine = pl.ds(pl.multiple_of(core * half, half), half)
    up_rows, low_rows = upper.shape[1], lower.shape[1]

    def own_up(k):
        return pltpu.make_async_copy(
            upper.at[k, :, mine], up.at[pl.ds(k * up_rows, up_rows), mine], inv_send.at[0, k]
        )

    def own_low(k):
        return pltpu.make_async_copy(
            lower.at[k], low.at[pl.ds(k * low_rows, low_rows)], inv_send.at[1, k]
        )

    def up_has(source):
        return (source + 1) * up_rows > core * half

    for k in range(2):

        @pl.when((c == k) & up_has(k))
        def _():
            own_up(k).start()

        @pl.when(r == k)
        def _():
            own_low(k).start()

    lanes = lax.broadcasted_iota(jnp.int32, (1, width), 1)

    def keep(a, b):
        return (lanes < ranks[a, b]).astype(jnp.float32).astype(jnp.bfloat16)

    def col_slot(kind, k, t):
        return 2 * t + kind if k == 0 else 2 * kind + t

    def row_slot(kind, k, t):
        return 2 * (1 - kind) + t if k == 0 else 2 * kind + t

    def col_wanted(k, slot):
        t = slot // 2 if k == 0 else slot % 2
        return True if t > 0 else r > k

    def row_wanted(k, slot):
        return True if slot % 2 > 0 or (k, slot) == (0, 2) else c > k

    def piece(q):
        return pl.ds(pl.multiple_of(q * step, step), step)

    def col_copy(k, slot, q, way, target):
        view = colb.at[k, slot] if q is None else colb.at[k, slot, piece(q)]
        return pltpu.make_async_remote_copy(
            src_ref=view,
            dst_ref=view,
            send_sem=col_send.at[k, slot, way],
            recv_sem=col_recv.at[k, slot, 0 if q is None else q],
            device_id={"col": target},
            device_id_type=MESH,
        )

    def row_copy(k, slot, q, way, target):
        view = rowb.at[k, slot] if q is None else rowb.at[k, slot, piece(q)]
        return pltpu.make_async_remote_copy(
            src_ref=view,
            dst_ref=view,
            send_sem=row_send.at[k, slot, way],
            recv_sem=row_recv.at[k, slot, 0 if q is None else q],
            device_id={"row": target},
            device_id_type=MESH,
        )

    def col_ways(k):
        return [
            ((x == k) & (c + minor_col < n_col), c + minor_col),
            ((x >= k) & (x + 1 < minor_col), c + 1),
            ((x <= k) & (x >= 1), c - 1),
        ]

    def row_ways():
        return [(r + 2 < n_row, r + 2), (r >= 0, r + 1 - 2 * core)]

    def col_forward(k, slot, q, ways=(0, 1, 2)):
        for way in ways:
            needed, target = col_ways(k)[way]

            @pl.when(needed)
            def _():
                col_copy(k, slot, q, way, target).start()

    def row_forward(k, slot, q):
        for way, (needed, target) in enumerate(row_ways()):

            @pl.when(needed)
            def _():
                row_copy(k, slot, q, way, target).start()

    def col_send_out(k, slot, ways=(0, 1, 2)):
        @pl.when((c == k) & col_wanted(k, slot))
        def _():
            @pl.loop(0, CHUNKS)
            def _(q):
                col_forward(k, slot, q, ways)

    def row_send_out(k, slot):
        @pl.when((r == k) & row_wanted(k, slot))
        def _():
            @pl.loop(0, CHUNKS)
            def _(q):
                row_forward(k, slot, q)

    trunk = jnp.minimum(x, 1)

    def col_relay_piece(slot, q):
        col_copy(trunk, slot, q, 0, 0).wait_recv()
        col_forward(trunk, slot, q)

    def col_relay(slot, also):
        @pl.when((c >= 2) & (x < 2) & also)
        def _():
            @pl.loop(0, CHUNKS)
            def _(q):
                col_relay_piece(slot, q)

    def row_relay_piece(slot, q):
        row_copy(core, slot, q, 0, 0).wait_recv()
        row_forward(core, slot, q)

    def row_relay(slot, also):
        @pl.when((r >= 2) & also)
        def _():
            @pl.loop(0, CHUNKS)
            def _(q):
                row_relay_piece(slot, q)

    def col_leaf(k, *slots, also=True):
        for slot in slots:

            @pl.when((x != k) & col_wanted(k, slot) & also)
            def _():
                @pl.loop(0, CHUNKS)
                def _(q):
                    col_copy(k, slot, q, 0, 0).wait_recv()
                    if minor_col > 2:
                        col_forward(k, slot, q, (1, 2))

    def row_leaf(k, *slots, also=True):
        for slot in slots:

            @pl.when((core != k) & row_wanted(k, slot) & also)
            def _():
                @pl.loop(0, CHUNKS)
                def _(q):
                    row_copy(k, slot, q, 0, 0).wait_recv()

    def swap_halves():
        return pltpu.make_async_remote_copy(
            src_ref=up.at[:, mine],
            dst_ref=up.at[:, mine],
            send_sem=swap_sem.at[0],
            recv_sem=swap_sem.at[1],
            device_id={"row": r + 1 - 2 * core},
            device_id_type=MESH,
        )

    def up_copy(k, source):
        return pltpu.make_async_remote_copy(
            src_ref=upper.at[k, :, mine],
            dst_ref=up.at[pl.ds(pl.multiple_of(source * up_rows, up_rows), up_rows), mine],
            send_sem=inv_send.at[0, k],
            recv_sem=up_recv.at[source],
            device_id={"col": k},
            device_id_type=MESH,
        )

    def low_copy(k, source):
        return pltpu.make_async_remote_copy(
            src_ref=lower.at[k],
            dst_ref=low.at[pl.ds(pl.multiple_of(source * low_rows, low_rows), low_rows)],
            send_sem=inv_send.at[1, k],
            recv_sem=low_recv.at[source],
            device_id={"row": k},
            device_id_type=MESH,
        )

    def lend_left():
        return pltpu.make_async_remote_copy(
            src_ref=ul.at[0, 0],
            dst_ref=colb.at[0, 0],
            send_sem=extra_sem.at[0],
            recv_sem=extra_sem.at[1],
            device_id={"col": 0},
            device_id_type=MESH,
        )

    def pass_mixed():
        return pltpu.make_async_remote_copy(
            src_ref=mix,
            dst_ref=mix,
            send_sem=extra_sem.at[2],
            recv_sem=extra_sem.at[3],
            device_id={"col": 1},
            device_id_type=MESH,
        )

    U, Y = 0, 1

    for a, b in every:
        fetch_left[a][b].wait()
        ul[a, b] = ul[a, b] * keep(a, b)
        if b == 0:
            for k in range(2):
                slot = col_slot(U, k, a)

                @pl.when((c == k) & col_wanted(k, slot))
                def _():
                    colb[k, slot] = ul[a, 0]

    for a, b in every:
        fetch_right[a][b].wait()
        out[a, b] = out[a, b] * keep(a, b)
        if a == 0:

            @pl.when(r == 0)
            def _():
                rowb[0, row_slot(Y, 0, b)] = out[0, b]

    pl.semaphore_wait(barrier, greeted)

    def give_up(k):
        @pl.when((c != k) & up_has(c))
        def _():
            up_copy(k, c).start()

    give_up(0)
    for k in range(2):

        @pl.when(r != k)
        def _():
            low_copy(k, r).start()

    def core_of(panel, a, b):
        return matmul_tn(
            colb[panel, col_slot(Y, panel, a)], rowb[panel, row_slot(U, panel, b)]
        ).astype(jnp.bfloat16)

    def subtract(panel, a, b, mixed):
        change = matmul_nt(rowb[panel, row_slot(Y, panel, b)], mixed)
        out[a, b] = (out[a, b].astype(jnp.float32) - change).astype(jnp.bfloat16)

    def update(panel, a, b, also=True):
        @pl.when((True if a > 0 else r > panel) & also)
        def _():
            meet = matmul_tn(ul[a, b], colb[panel, col_slot(U, panel, a)]).astype(jnp.bfloat16)
            mixed = matmul(meet, core_of(panel, a, b)).astype(jnp.bfloat16)
            subtract(panel, a, b, mixed)

    def wait_low(k):
        own_low(k).wait()
        for s in range(n_row):
            if s != k:
                low_copy(k, s).wait_recv()

    def solve_row(k, b, source=None):
        slot = row_slot(U, k, b)
        rowb[k, slot] = matmul(low[...], ul[0, b] if source is None else source[...]).astype(jnp.bfloat16)

    def solve_col(k, a):
        colb[k, col_slot(Y, k, a)] = matmul(up[...], out[a, 0]).astype(jnp.bfloat16)

    def share_row(b):
        rowb[1, row_slot(Y, 1, b)] = out[0, b]
        row_send_out(1, row_slot(Y, 1, b))

    even, odd = (r >= 2) & (core == 0), (r >= 2) & (core == 1)

    @pl.when(r == 0)
    def _():
        row_send_out(0, 0)
        row_send_out(0, 1)

    @pl.when(c < 2)
    def _():
        @pl.when((c == 1) & (r == 0))
        def _():
            lend_left().start()

        col_send_out(0, 0)
        col_send_out(1, 1, (1, 2))
        col_send_out(1, 0, (0,))
        col_send_out(1, 1, (0,))
        col_send_out(1, 0, (1, 2))

        @pl.when(r == 0)
        def _():
            wait_low(0)

            @pl.when(c == 0)
            def _():
                lend_left().wait_recv()
                solve_row(0, 0, colb.at[0, 0])

            @pl.when(c != 0)
            def _():
                solve_row(0, 0)

            row_send_out(0, 2)
            solve_row(0, 1)
            row_send_out(0, 3)

        give_up(1)
        for k in range(2):

            @pl.when((c == k) & up_has(k))
            def _():
                own_up(k).wait()

        for s in range(n_col):

            @pl.when((s != c) & up_has(s))
            def _():
                up_copy(0, s).wait_recv()

        swap_halves().start()
        swap_halves().wait_recv()

        @pl.when(c == 0)
        def _():
            @pl.when(r > 0)
            def _():
                solve_col(0, 0)

            col_send_out(0, 1)
            col_send_out(0, 2, (0,))
            solve_col(0, 1)
            col_send_out(0, 3, (0,))

        @pl.when(r == 1)
        def _():
            wait_low(1)
            solve_row(1, 1)
            row_send_out(1, 1)

        row_relay(0, even & (c == 1))
        row_relay(1, even)
        row_relay(2, even)
        row_leaf(0, 0, 2)

        @pl.when(c == 0)
        def _():
            col_leaf(1, 1)
            meet = matmul_tn(colb[1, col_slot(U, 1, 1)], ul[1, 0]).astype(jnp.bfloat16)
            mix[...] = matmul(meet, core_of(0, 1, 0)).astype(jnp.bfloat16)
            pass_mixed().start()
            col_send_out(0, 2, (1, 2))
            col_send_out(0, 3, (1, 2))

        @pl.when(c == 1)
        def _():
            col_leaf(0, 0, 1)
            update(0, 0, 0)

            @pl.when(r > 1)
            def _():
                solve_col(1, 0)

            col_send_out(1, 2)

        row_relay(3, even)
        row_leaf(0, 1, 3)
        update(0, 0, 1, also=r == 1)

        @pl.when(r == 1)
        def _():
            share_row(1)

        @pl.when(c == 1)
        def _():
            pass_mixed().wait_recv()
            subtract(0, 1, 0, mix[...])
            solve_col(1, 1)
            col_send_out(1, 3)

        row_relay(1, odd)
        update(0, 0, 1, also=r != 1)
        col_leaf(0, 2, 3)
        update(0, 1, 1)
        row_relay(3, odd)
        row_leaf(1, 1, 3)
        col_leaf(1, 0)
        col_leaf(1, 2)
        update(1, 0, 1)
        col_leaf(1, 3)
        update(1, 1, 1)
        for panel in range(2):
            for a in range(2):

                @pl.when((c == panel) & (True if a > 0 else r > panel))
                def _():
                    out[a, 0] = colb[panel, col_slot(Y, panel, a)]

    @pl.when((c >= 2) & (r < 2))
    def _():
        give_up(1)

        @pl.when(r == 0)
        def _():
            wait_low(0)
            for b in range(2):
                solve_row(0, b)
                row_send_out(0, 2 + b)

        col_relay(0, (r == 1) & (x == 0))
        col_relay(1, x == 1)
        col_relay(2, (r == 0) & (x == 0))

        @pl.when(r == 1)
        def _():
            wait_low(1)
            for b in range(2):
                solve_row(1, b)
                row_send_out(1, b)

            col_relay(1, x == 0)
            col_leaf(0, 0, 1)
            for b in range(2):
                row_leaf(0, b, 2 + b)
                update(0, 0, b)
                share_row(b)

            col_relay(2, x == 0)

        col_relay(3, r >= 0)
        col_leaf(0, 2, 3)
        update(0, 1, 0)
        update(0, 1, 1)
        col_leaf(1, 1, 3)
        for b in range(2):
            row_leaf(1, b, 2 + b)
            update(1, 1, b)

    @pl.when((c >= 2) & (r >= 2))
    def _():
        main = x < 2

        def pump(slot, even_rows, odd_rows, begin=0, end=CHUNKS):
            @pl.loop(begin, end)
            def _(q):
                @pl.when(main)
                def _():
                    col_relay_piece(slot, q)

                for role, rows in ((core == 0, even_rows), (core == 1, odd_rows)):
                    for first, rate in rows:
                        for extra in range(rate):

                            @pl.when(role)
                            def _():
                                m = first * CHUNKS + q * rate + extra
                                row_relay_piece(m // CHUNKS, lax.rem(m, CHUNKS))

        pump(0, [(0, 1)], [], end=CHUNKS // 4)
        give_up(1)
        pump(0, [(0, 1)], [], begin=CHUNKS // 4)
        pump(1, [(1, 2)], [])
        col_leaf(0, 0, 1)
        row_leaf(0, 0, 2)
        update(0, 0, 0)
        pump(2, [(3, 1)], [(0, 2)])
        row_leaf(0, 1, 3)
        update(0, 0, 1)
        pump(3, [], [(2, 2)])
        col_leaf(1, 0, 2)
        for b in range(2):
            row_leaf(1, b, 2 + b)
            update(1, 0, b)
        col_leaf(0, 2, 3)
        update(0, 1, 0)
        update(0, 1, 1)
        col_leaf(1, 1, 3)
        update(1, 1, 0)
        update(1, 1, 1)

    for k in range(2):

        @pl.when((c != k) & up_has(c))
        def _():
            up_copy(k, c).wait_send()

        @pl.when(r != k)
        def _():
            low_copy(k, r).wait_send()

    @pl.when(c < 2)
    def _():
        swap_halves().wait_send()

        @pl.when((c == 1) & (r == 0))
        def _():
            lend_left().wait_send()

        @pl.when(c == 0)
        def _():
            pass_mixed().wait_send()

    for k in range(2):
        for slot in range(4):
            for way, (needed, target) in enumerate(col_ways(k)):

                @pl.when(needed & col_wanted(k, slot))
                def _():
                    col_copy(k, slot, None, way, target).wait_send()

            for way, (needed, target) in enumerate(row_ways()):

                @pl.when((core == k) & needed & row_wanted(k, slot))
                def _():
                    row_copy(k, slot, None, way, target).wait_send()


def body(left, right, lower_inverse, upper_inverse, ranks):
    n_row, n_col = lax.axis_size("row"), lax.axis_size("col")
    minor_col = 4 if n_col % 4 == 0 and n_col > 8 else 2
    order, width = left.shape[2:]
    upper = jnp.swapaxes(upper_inverse, 1, 2)
    tile = (order, width)
    vmem = pl.BlockSpec(memory_space=pltpu.VMEM)
    hbm = pl.BlockSpec(memory_space=pltpu.HBM)
    return pl.pallas_call(
        functools.partial(kernel, n_row, n_col, minor_col),
        out_shape=jax.ShapeDtypeStruct(right.shape, jnp.bfloat16),
        in_specs=[pl.BlockSpec(memory_space=pltpu.SMEM)] + [hbm] * 4,
        out_specs=vmem,
        scratch_shapes=[
            pltpu.VMEM((2, 2) + tile, jnp.bfloat16),
            pltpu.VMEM((2, 4) + tile, jnp.bfloat16),
            pltpu.VMEM((2, 4) + tile, jnp.bfloat16),
            pltpu.VMEM((order, order), jnp.bfloat16),
            pltpu.VMEM((order, order), jnp.bfloat16),
            pltpu.VMEM((width, width), jnp.bfloat16),
            pltpu.SemaphoreType.DMA((2, 4, 3)),
            pltpu.SemaphoreType.DMA((2, 4, CHUNKS)),
            pltpu.SemaphoreType.DMA((2, 4, 2)),
            pltpu.SemaphoreType.DMA((2, 4, CHUNKS)),
            pltpu.SemaphoreType.DMA((2, 2)),
            pltpu.SemaphoreType.DMA((n_row,)),
            pltpu.SemaphoreType.DMA((n_col,)),
            pltpu.SemaphoreType.DMA((2, 2, 2)),
            pltpu.SemaphoreType.DMA((2,)),
            pltpu.SemaphoreType.DMA((4,)),
        ],
        compiler_params=pltpu.CompilerParams(
            collective_id=0, has_side_effects=True, vmem_limit_bytes=60 * 1024 * 1024
        ),
        cost_estimate=pl.CostEstimate(
            flops=2_000_000_000, bytes_accessed=4_000_000, transcendentals=0
        ),
    )(ranks, left, right, lower_inverse, upper)


def solution(mesh):
    placed = (
        P("row", "col", None, None),
        P("row", "col", None, None),
        P(None, "row", None),
        P(None, None, "col"),
        P("row", "col"),
    )
    return jax.shard_map(
        body, mesh=mesh, in_specs=placed, out_specs=P("row", "col", None, None), check_vma=False
    )
```

```python
import functools

import jax
import jax.numpy as jnp
from jax import lax
from jax.experimental import pallas as pl
from jax.experimental.pallas import tpu as pltpu
from jax.sharding import PartitionSpec as P

CHUNKS = 8
MESH = pl.DeviceIdType.MESH
UP, ALONG = (0, 1, 2), (3, 4)
ALL = UP + ALONG


def matmul(a, b):
    return jnp.dot(a, b, preferred_element_type=jnp.float32)


def matmul_tn(a, b):
    return lax.dot_general(a, b, (((0,), (0,)), ((), ())), preferred_element_type=jnp.float32)


def matmul_nt(a, b):
    return lax.dot_general(a, b, (((1,), (1,)), ((), ())), preferred_element_type=jnp.float32)


def kernel(
    n_row, n_col, minor_col, ranks, left, right, lower, upper, out,
    ul, colb, rowb, low, up, mix, part,
    col_send, col_recv, row_send, row_recv, inv_send, low_recv, up_recv, fetch_sem, swap_sem, extra_sem,
):
    r, c = lax.axis_index("row"), lax.axis_index("col")
    x, core = lax.rem(c, minor_col), lax.rem(r, 2)
    order, width = left.shape[2], left.shape[3]
    step = order // CHUNKS
    fetch_left = [
        [pltpu.make_async_copy(left.at[a, b], ul.at[a, b], fetch_sem.at[0, a, b]) for b in range(2)]
        for a in range(2)
    ]
    fetch_right = [
        [pltpu.make_async_copy(right.at[a, b], out.at[a, b], fetch_sem.at[1, a, b]) for b in range(2)]
        for a in range(2)
    ]
    every = [(0, 0), (1, 0), (0, 1), (1, 1)]
    for a, b in every:
        fetch_left[a][b].start()
    for a, b in every:
        fetch_right[a][b].start()

    @pl.when(c < 2)
    def _():
        up[...] = jnp.zeros_like(up)

    barrier = pltpu.get_barrier_semaphore()

    def greet(needed, **target):
        @pl.when(needed)
        def _():
            pl.semaphore_signal(barrier, inc=1, device_id=target, device_id_type=MESH)

    def count(*needed):
        return sum(flag.astype(jnp.int32) for flag in needed)

    depth = n_col // minor_col
    z = lax.div(c, minor_col)
    even_z = lax.rem(z, 2) == 0
    if depth > 2:
        skip, rise, fall = even_z & (z + 2 < depth), even_z & (z >= 2) & (z + 1 < depth), z == 2
        greet(even_z & (z >= 2), col=c - 2 * minor_col)
        greet(jnp.logical_not(even_z) & (z >= 3), col=c - minor_col)
        greet(z == 1, col=c + minor_col)
    else:
        skip, rise, fall = z < 0, z + 1 < depth, z < 0
        greet(z >= 1, col=c - minor_col)
    greet(r >= 2, row=r - 2)
    greet(r >= 0, row=r + 1 - 2 * core)
    greet(x + 1 < minor_col, col=c + 1)
    greet(x >= 1, col=c - 1)
    for d in range(1, n_row):
        greet(r < 2, row=lax.rem(r + d, n_row))
    for d in range(1, n_col):
        greet(c < 2, col=lax.rem(c + d, n_col))
    greeted = 1 + count(
        r + 2 < n_row, x + 1 < minor_col, x >= 1, skip, rise, fall, r != 0, r != 1, c != 0, c != 1
    )

    half = order // 2
    mine = pl.ds(pl.multiple_of(core * half, half), half)
    up_rows, low_rows = upper.shape[1], lower.shape[1]

    def own_up(k):
        return pltpu.make_async_copy(
            upper.at[k, :, mine], up.at[pl.ds(k * up_rows, up_rows), mine], inv_send.at[0, k]
        )

    def own_low(k):
        return pltpu.make_async_copy(
            lower.at[k], low.at[pl.ds(k * low_rows, low_rows)], inv_send.at[1, k]
        )

    def up_has(source):
        return (source + 1) * up_rows > core * half

    for k in range(2):

        @pl.when((c == k) & up_has(k))
        def _():
            own_up(k).start()

        @pl.when(r == k)
        def _():
            own_low(k).start()

    lanes = lax.broadcasted_iota(jnp.int32, (1, width), 1)

    def keep(a, b):
        return (lanes < ranks[a, b]).astype(jnp.float32).astype(jnp.bfloat16)

    def col_slot(kind, k, t):
        return 2 * t + kind if k == 0 else 2 * kind + t

    def row_slot(kind, k, t):
        return 2 * (1 - kind) + t if k == 0 else 2 * kind + t

    def col_wanted(k, slot):
        t = slot // 2 if k == 0 else slot % 2
        return True if t > 0 else r > k

    def row_wanted(k, slot):
        return True if slot % 2 > 0 or (k, slot) == (0, 2) else c > k

    def piece(q):
        return pl.ds(pl.multiple_of(q * step, step), step)

    def col_copy(k, slot, q, way, target):
        view = colb.at[k, slot] if q is None else colb.at[k, slot, piece(q)]
        return pltpu.make_async_remote_copy(
            src_ref=view,
            dst_ref=view,
            send_sem=col_send.at[k, slot, way],
            recv_sem=col_recv.at[k, slot, 0 if q is None else q],
            device_id={"col": target},
            device_id_type=MESH,
        )

    def row_copy(k, slot, q, way, target):
        view = rowb.at[k, slot] if q is None else rowb.at[k, slot, piece(q)]
        return pltpu.make_async_remote_copy(
            src_ref=view,
            dst_ref=view,
            send_sem=row_send.at[k, slot, way],
            recv_sem=row_recv.at[k, slot, 0 if q is None else q],
            device_id={"row": target},
            device_id_type=MESH,
        )

    def col_ways(k):
        return [
            ((x == k) & skip, c + 2 * minor_col),
            ((x == k) & rise, c + minor_col),
            ((x == k) & fall, c - minor_col),
            ((x >= k) & (x + 1 < minor_col), c + 1),
            ((x <= k) & (x >= 1), c - 1),
        ]

    def row_ways():
        return [(r + 2 < n_row, r + 2), (r >= 0, r + 1 - 2 * core)]

    def col_forward(k, slot, q, ways=ALL):
        for way in ways:
            needed, target = col_ways(k)[way]

            @pl.when(needed)
            def _():
                col_copy(k, slot, q, way, target).start()

    def row_forward(k, slot, q):
        for way, (needed, target) in enumerate(row_ways()):

            @pl.when(needed)
            def _():
                row_copy(k, slot, q, way, target).start()

    def col_send_out(k, slot, ways=ALL):
        @pl.when((c == k) & col_wanted(k, slot))
        def _():
            @pl.loop(0, CHUNKS)
            def _(q):
                col_forward(k, slot, q, ways)

    def row_send_out(k, slot):
        @pl.when((r == k) & row_wanted(k, slot))
        def _():
            @pl.loop(0, CHUNKS)
            def _(q):
                row_forward(k, slot, q)

    trunk = jnp.minimum(x, 1)

    def col_relay_piece(slot, q):
        col_copy(trunk, slot, q, 0, 0).wait_recv()
        col_forward(trunk, slot, q)

    def col_relay(slot, also):
        @pl.when((c >= 2) & (x < 2) & also)
        def _():
            @pl.loop(0, CHUNKS)
            def _(q):
                col_relay_piece(slot, q)

    def row_relay_piece(slot, q):
        row_copy(core, slot, q, 0, 0).wait_recv()
        row_forward(core, slot, q)

    def row_relay(slot, also):
        @pl.when((r >= 2) & also)
        def _():
            @pl.loop(0, CHUNKS)
            def _(q):
                row_relay_piece(slot, q)

    def col_leaf(k, *slots, also=True):
        for slot in slots:

            @pl.when((x != k) & col_wanted(k, slot) & also)
            def _():
                @pl.loop(0, CHUNKS)
                def _(q):
                    col_copy(k, slot, q, 0, 0).wait_recv()
                    if minor_col > 2:
                        col_forward(k, slot, q, ALONG)

    def row_leaf(k, *slots, also=True):
        for slot in slots:

            @pl.when((core != k) & row_wanted(k, slot) & also)
            def _():
                @pl.loop(0, CHUNKS)
                def _(q):
                    row_copy(k, slot, q, 0, 0).wait_recv()

    def swap_halves():
        return pltpu.make_async_remote_copy(
            src_ref=up.at[:, mine],
            dst_ref=up.at[:, mine],
            send_sem=swap_sem.at[0],
            recv_sem=swap_sem.at[1],
            device_id={"row": r + 1 - 2 * core},
            device_id_type=MESH,
        )

    def up_copy(k, source):
        return pltpu.make_async_remote_copy(
            src_ref=upper.at[k, :, mine],
            dst_ref=up.at[pl.ds(pl.multiple_of(source * up_rows, up_rows), up_rows), mine],
            send_sem=inv_send.at[0, k],
            recv_sem=up_recv.at[source],
            device_id={"col": k},
            device_id_type=MESH,
        )

    def low_copy(k, source):
        return pltpu.make_async_remote_copy(
            src_ref=lower.at[k],
            dst_ref=low.at[pl.ds(pl.multiple_of(source * low_rows, low_rows), low_rows)],
            send_sem=inv_send.at[1, k],
            recv_sem=low_recv.at[source],
            device_id={"row": k},
            device_id_type=MESH,
        )

    def lend_left():
        return pltpu.make_async_remote_copy(
            src_ref=ul.at[0, 0],
            dst_ref=colb.at[0, 0],
            send_sem=extra_sem.at[0],
            recv_sem=extra_sem.at[1],
            device_id={"col": 0},
            device_id_type=MESH,
        )

    def pass_mixed():
        return pltpu.make_async_remote_copy(
            src_ref=mix,
            dst_ref=mix,
            send_sem=extra_sem.at[2],
            recv_sem=extra_sem.at[3],
            device_id={"col": 1},
            device_id_type=MESH,
        )

    U, Y = 0, 1

    for a, b in every:
        fetch_left[a][b].wait()
        ul[a, b] = ul[a, b] * keep(a, b)
        if b == 0:
            for k in range(2):
                slot = col_slot(U, k, a)

                @pl.when((c == k) & col_wanted(k, slot))
                def _():
                    colb[k, slot] = ul[a, 0]

    for a, b in every:
        fetch_right[a][b].wait()
        out[a, b] = out[a, b] * keep(a, b)
        if a == 0:

            @pl.when(r == 0)
            def _():
                rowb[0, row_slot(Y, 0, b)] = out[0, b]

    pl.semaphore_wait(barrier, greeted)

    def give_up(k):
        @pl.when((c != k) & up_has(c))
        def _():
            up_copy(k, c).start()

    give_up(0)
    for k in range(2):

        @pl.when(r != k)
        def _():
            low_copy(k, r).start()

    def core_of(panel, a, b):
        return matmul_tn(
            colb[panel, col_slot(Y, panel, a)], rowb[panel, row_slot(U, panel, b)]
        ).astype(jnp.bfloat16)

    def meet_of(panel, a, b):
        return matmul_tn(ul[a, b], colb[panel, col_slot(U, panel, a)]).astype(jnp.bfloat16)

    def subtract(panel, a, b, mixed):
        change = matmul_nt(rowb[panel, row_slot(Y, panel, b)], mixed)
        out[a, b] = (out[a, b].astype(jnp.float32) - change).astype(jnp.bfloat16)

    def update(panel, a, b, also=True):
        @pl.when((True if a > 0 else r > panel) & also)
        def _():
            mixed = matmul(meet_of(panel, a, b), core_of(panel, a, b)).astype(jnp.bfloat16)
            subtract(panel, a, b, mixed)

    def meet(panel, a, b):
        part[panel, a, b] = meet_of(panel, a, b)

    def blend(panel, a, b):
        part[panel, a, b] = matmul(part[panel, a, b], core_of(panel, a, b)).astype(jnp.bfloat16)

    def apply(panel, a, b):
        subtract(panel, a, b, part[panel, a, b])

    def wait_low(k):
        own_low(k).wait()
        for s in range(n_row):
            if s != k:
                low_copy(k, s).wait_recv()

    def solve_row(k, b, source=None):
        slot = row_slot(U, k, b)
        rowb[k, slot] = matmul(low[...], ul[0, b] if source is None else source[...]).astype(jnp.bfloat16)

    def solve_col(k, a):
        colb[k, col_slot(Y, k, a)] = matmul(up[...], out[a, 0]).astype(jnp.bfloat16)

    def share_row(b):
        rowb[1, row_slot(Y, 1, b)] = out[0, b]
        row_send_out(1, row_slot(Y, 1, b))

    even, odd = (r >= 2) & (core == 0), (r >= 2) & (core == 1)

    @pl.when(r == 0)
    def _():
        row_send_out(0, 0)
        row_send_out(0, 1)

    @pl.when(c < 2)
    def _():
        @pl.when((c == 1) & (r == 0))
        def _():
            lend_left().start()

        col_send_out(0, 0)
        col_send_out(1, 1, ALONG)
        col_send_out(1, 0, UP)
        col_send_out(1, 1, UP)
        col_send_out(1, 0, ALONG)

        @pl.when(r == 0)
        def _():
            wait_low(0)

            @pl.when(c == 0)
            def _():
                lend_left().wait_recv()
                solve_row(0, 0, colb.at[0, 0])

            @pl.when(c != 0)
            def _():
                solve_row(0, 0)

            row_send_out(0, 2)
            solve_row(0, 1)
            row_send_out(0, 3)

        give_up(1)
        for k in range(2):

            @pl.when((c == k) & up_has(k))
            def _():
                own_up(k).wait()

        for s in range(n_col):

            @pl.when((s != c) & up_has(s))
            def _():
                up_copy(0, s).wait_recv()

        swap_halves().start()
        swap_halves().wait_recv()

        @pl.when(c == 0)
        def _():
            @pl.when(r > 0)
            def _():
                solve_col(0, 0)

            col_send_out(0, 1)
            col_send_out(0, 2, UP)
            solve_col(0, 1)
            col_send_out(0, 3, UP)

        @pl.when(r == 1)
        def _():
            wait_low(1)
            solve_row(1, 1)
            row_send_out(1, 1)

        row_relay(0, even & (c == 1))
        row_relay(1, even)
        row_relay(2, even)
        row_leaf(0, 0, 2)

        @pl.when(c == 0)
        def _():
            col_leaf(1, 1)
            crossed = matmul_tn(colb[1, col_slot(U, 1, 1)], ul[1, 0]).astype(jnp.bfloat16)
            mix[...] = matmul(crossed, core_of(0, 1, 0)).astype(jnp.bfloat16)
            pass_mixed().start()
            col_send_out(0, 2, ALONG)
            col_send_out(0, 3, ALONG)

        @pl.when(c == 1)
        def _():
            col_leaf(0, 0, 1)
            update(0, 0, 0)

            @pl.when(r > 1)
            def _():
                solve_col(1, 0)

            col_send_out(1, 2)

        row_relay(3, even)
        row_leaf(0, 1, 3)
        update(0, 0, 1, also=r == 1)

        @pl.when(r == 1)
        def _():
            share_row(1)

        @pl.when(c == 1)
        def _():
            pass_mixed().wait_recv()
            subtract(0, 1, 0, mix[...])
            solve_col(1, 1)
            col_send_out(1, 3)

        row_relay(1, odd)
        update(0, 0, 1, also=r != 1)
        col_leaf(0, 2, 3)
        update(0, 1, 1)
        row_relay(3, odd)
        row_leaf(1, 1, 3)
        col_leaf(1, 0)
        col_leaf(1, 2)
        update(1, 0, 1)
        col_leaf(1, 3)
        update(1, 1, 1)
        for panel in range(2):
            for a in range(2):

                @pl.when((c == panel) & (True if a > 0 else r > panel))
                def _():
                    out[a, 0] = colb[panel, col_slot(Y, panel, a)]

    @pl.when((c >= 2) & (r < 2))
    def _():
        give_up(1)

        @pl.when(r == 0)
        def _():
            wait_low(0)
            for b in range(2):
                solve_row(0, b)
                row_send_out(0, 2 + b)

        col_relay(0, (r == 1) & (x == 0))
        col_relay(1, x == 1)
        col_relay(2, (r == 0) & (x == 0))

        @pl.when(r == 1)
        def _():
            wait_low(1)
            for b in range(2):
                solve_row(1, b)
                row_send_out(1, b)

            col_relay(1, x == 0)
            col_leaf(0, 0, 1)
            for b in range(2):
                row_leaf(0, b, 2 + b)
                update(0, 0, b)
                share_row(b)

            col_relay(2, x == 0)

        col_relay(3, x == 0)
        col_leaf(0, 2)
        col_leaf(1, 1)
        for panel in range(2):
            for b in range(2):
                meet(panel, 1, b)
        col_relay(3, x == 1)
        col_leaf(0, 3)
        for b in range(2):
            blend(0, 1, b)
            apply(0, 1, b)
        row_leaf(1, 0, 1, 2, 3)
        col_leaf(1, 3)
        for b in range(2):
            blend(1, 1, b)
            apply(1, 1, b)

    @pl.when((c >= 2) & (r >= 2))
    def _():
        main = x < 2

        def pump(slot, even_rows, odd_rows, begin=0, end=CHUNKS):
            @pl.loop(begin, end)
            def _(q):
                @pl.when(main)
                def _():
                    col_relay_piece(slot, q)

                for role, rows in ((core == 0, even_rows), (core == 1, odd_rows)):
                    for first, rate in rows:
                        for extra in range(rate):

                            @pl.when(role)
                            def _():
                                m = first * CHUNKS + q * rate + extra
                                row_relay_piece(m // CHUNKS, lax.rem(m, CHUNKS))

        pump(0, [(0, 1)], [], end=CHUNKS // 4)
        give_up(1)
        pump(0, [(0, 1)], [], begin=CHUNKS // 4)
        def pump_beside(slot, even_rows, odd_rows, jobs):
            for q in range(CHUNKS):
                pump(slot, even_rows, odd_rows, q, q + 1)
                if q < len(jobs) and jobs[q] is not None:
                    jobs[q]()

        def last_meet():
            col_leaf(0, 2)
            meet(0, 1, 0)

        def next_blend():
            col_leaf(1, 2)
            row_leaf(1, 0)
            blend(1, 0, 0)

        def last_blend():
            row_leaf(1, 1)
            blend(1, 0, 1)

        pump(1, [(1, 2)], [])
        col_leaf(0, 0, 1)
        row_leaf(0, 0, 2)
        col_leaf(1, 0, 1)
        at = functools.partial
        pump_beside(
            2,
            [(3, 1)],
            [(0, 2)],
            [
                at(meet, 0, 0, 0),
                at(blend, 0, 0, 0),
                at(apply, 0, 0, 0),
                at(meet, 0, 0, 1),
                at(meet, 1, 0, 0),
                at(meet, 1, 0, 1),
                at(meet, 1, 1, 0),
                at(meet, 1, 1, 1),
            ],
        )
        row_leaf(0, 1, 3)
        pump_beside(
            3,
            [],
            [(2, 2)],
            [
                at(blend, 0, 0, 1),
                at(apply, 0, 0, 1),
                None,
                last_meet,
                at(meet, 0, 1, 1),
                None,
                next_blend,
                last_blend,
            ],
        )
        for b in range(2):
            row_leaf(1, 2 + b)
            apply(1, 0, b)
        col_leaf(0, 3)
        for b in range(2):
            blend(0, 1, b)
            apply(0, 1, b)
        col_leaf(1, 3)
        for b in range(2):
            blend(1, 1, b)
            apply(1, 1, b)

    for k in range(2):

        @pl.when((c != k) & up_has(c))
        def _():
            up_copy(k, c).wait_send()

        @pl.when(r != k)
        def _():
            low_copy(k, r).wait_send()

    @pl.when(c < 2)
    def _():
        swap_halves().wait_send()

        @pl.when((c == 1) & (r == 0))
        def _():
            lend_left().wait_send()

        @pl.when(c == 0)
        def _():
            pass_mixed().wait_send()

    for k in range(2):
        for slot in range(4):
            for way, (needed, target) in enumerate(col_ways(k)):

                @pl.when(needed & col_wanted(k, slot))
                def _():
                    col_copy(k, slot, None, way, target).wait_send()

            for way, (needed, target) in enumerate(row_ways()):

                @pl.when((core == k) & needed & row_wanted(k, slot))
                def _():
                    row_copy(k, slot, None, way, target).wait_send()


def body(left, right, lower_inverse, upper_inverse, ranks):
    n_row, n_col = lax.axis_size("row"), lax.axis_size("col")
    minor_col = 4 if n_col % 4 == 0 and n_col > 8 else 2
    order, width = left.shape[2:]
    upper = jnp.swapaxes(upper_inverse, 1, 2)
    tile = (order, width)
    vmem = pl.BlockSpec(memory_space=pltpu.VMEM)
    hbm = pl.BlockSpec(memory_space=pltpu.HBM)
    return pl.pallas_call(
        functools.partial(kernel, n_row, n_col, minor_col),
        out_shape=pltpu.VMEM(right.shape, jnp.bfloat16),
        in_specs=[pl.BlockSpec(memory_space=pltpu.SMEM)] + [hbm] * 4,
        out_specs=vmem,
        scratch_shapes=[
            pltpu.VMEM((2, 2) + tile, jnp.bfloat16),
            pltpu.VMEM((2, 4) + tile, jnp.bfloat16),
            pltpu.VMEM((2, 4) + tile, jnp.bfloat16),
            pltpu.VMEM((order, order), jnp.bfloat16),
            pltpu.VMEM((order, order), jnp.bfloat16),
            pltpu.VMEM((width, width), jnp.bfloat16),
            pltpu.VMEM((2, 2, 2, width, width), jnp.bfloat16),
            pltpu.SemaphoreType.DMA((2, 4, 5)),
            pltpu.SemaphoreType.DMA((2, 4, CHUNKS)),
            pltpu.SemaphoreType.DMA((2, 4, 2)),
            pltpu.SemaphoreType.DMA((2, 4, CHUNKS)),
            pltpu.SemaphoreType.DMA((2, 2)),
            pltpu.SemaphoreType.DMA((n_row,)),
            pltpu.SemaphoreType.DMA((n_col,)),
            pltpu.SemaphoreType.DMA((2, 2, 2)),
            pltpu.SemaphoreType.DMA((2,)),
            pltpu.SemaphoreType.DMA((4,)),
        ],
        compiler_params=pltpu.CompilerParams(
            collective_id=0, has_side_effects=True, vmem_limit_bytes=60 * 1024 * 1024
        ),
        cost_estimate=pl.CostEstimate(
            flops=2_000_000_000, bytes_accessed=4_000_000, transcendentals=0
        ),
    )(ranks, left, right, lower_inverse, upper)


def solution(mesh):
    placed = (
        P("row", "col", None, None),
        P("row", "col", None, None),
        P(None, "row", None),
        P(None, None, "col"),
        P("row", "col"),
    )
    return jax.shard_map(
        body, mesh=mesh, in_specs=placed, out_specs=P("row", "col", None, None), check_vma=False
    )
```

```python
import functools

import jax
import jax.numpy as jnp
from jax import lax
from jax.experimental import pallas as pl
from jax.experimental.pallas import tpu as pltpu
from jax.sharding import PartitionSpec as P

CHUNKS = 8
MESH = pl.DeviceIdType.MESH
UP, ALONG = (0, 1, 2), (3, 4)
ALL = UP + ALONG


def matmul(a, b):
    return jnp.dot(a, b, preferred_element_type=jnp.float32)


def matmul_tn(a, b):
    return lax.dot_general(a, b, (((0,), (0,)), ((), ())), preferred_element_type=jnp.float32)


def matmul_nt(a, b):
    return lax.dot_general(a, b, (((1,), (1,)), ((), ())), preferred_element_type=jnp.float32)


def kernel(
    n_row, n_col, minor_col, ranks, left, right, lower, upper, out,
    ul, colb, rowb, low, up, mix, part,
    col_send, col_recv, row_send, row_recv, inv_send, low_recv, up_recv, fetch_sem, swap_sem, extra_sem,
):
    r, c = lax.axis_index("row"), lax.axis_index("col")
    x, core = lax.rem(c, minor_col), lax.rem(r, 2)
    order, width = left.shape[2], left.shape[3]
    step = order // CHUNKS
    fetch_left = [
        [pltpu.make_async_copy(left.at[a, b], ul.at[a, b], fetch_sem.at[0, a, b]) for b in range(2)]
        for a in range(2)
    ]
    fetch_right = [
        [pltpu.make_async_copy(right.at[a, b], out.at[a, b], fetch_sem.at[1, a, b]) for b in range(2)]
        for a in range(2)
    ]
    @pl.when(c < 2)
    def _():
        up[...] = jnp.zeros_like(up)

    barrier = pltpu.get_barrier_semaphore()

    def greet(needed, **target):
        @pl.when(needed)
        def _():
            pl.semaphore_signal(barrier, inc=1, device_id=target, device_id_type=MESH)

    def count(*needed):
        return sum(flag.astype(jnp.int32) for flag in needed)

    for d in range(n_col - 1, 0, -1):
        greet(c < 2, col=lax.rem(c + d, n_col))
    for d in range(1, n_row):
        greet(r < 2, row=lax.rem(r + d, n_row))
    depth = n_col // minor_col
    z = lax.div(c, minor_col)
    even_z = lax.rem(z, 2) == 0
    if depth > 2:
        skip, rise, fall = even_z & (z + 2 < depth), even_z & (z >= 2) & (z + 1 < depth), z == 2
        greet(even_z & (z >= 2), col=c - 2 * minor_col)
        greet(jnp.logical_not(even_z) & (z >= 3), col=c - minor_col)
        greet(z == 1, col=c + minor_col)
    else:
        skip, rise, fall = z < 0, z + 1 < depth, z < 0
        greet(z >= 1, col=c - minor_col)
    greet(r >= 2, row=r - 2)
    greet(r >= 0, row=r + 1 - 2 * core)
    greet(x + 1 < minor_col, col=c + 1)
    greet(x >= 1, col=c - 1)
    greeted = 1 + count(
        r + 2 < n_row, x + 1 < minor_col, x >= 1, skip, rise, fall, r != 0, r != 1, c != 0, c != 1
    )

    for a in range(2):
        fetch_left[a][0].start()
    for b in range(2):
        fetch_right[0][b].start()
    for a in range(2):
        fetch_left[a][1].start()
    for b in range(2):
        fetch_right[1][b].start()

    half = order // 2
    mine = pl.ds(pl.multiple_of(core * half, half), half)
    up_rows, low_rows = upper.shape[1], lower.shape[1]

    def own_up(k):
        return pltpu.make_async_copy(
            upper.at[k, :, mine], up.at[pl.ds(k * up_rows, up_rows), mine], inv_send.at[0, k]
        )

    def own_low(k):
        return pltpu.make_async_copy(
            lower.at[k], low.at[pl.ds(k * low_rows, low_rows)], inv_send.at[1, k]
        )

    def up_has(source):
        return (source + 1) * up_rows > core * half

    for k in range(2):

        @pl.when((c == k) & up_has(k))
        def _():
            own_up(k).start()

        @pl.when(r == k)
        def _():
            own_low(k).start()

    lanes = lax.broadcasted_iota(jnp.int32, (1, width), 1)

    def keep(a, b):
        return (lanes < ranks[a, b]).astype(jnp.float32).astype(jnp.bfloat16)

    def col_slot(kind, k, t):
        return 2 * t + kind if k == 0 else 2 * kind + t

    def row_slot(kind, k, t):
        return 2 * (1 - kind) + t if k == 0 else 2 * kind + t

    def col_wanted(k, slot):
        t = slot // 2 if k == 0 else slot % 2
        return True if t > 0 else r > k

    def row_wanted(k, slot):
        return True if slot % 2 > 0 or (k, slot) == (0, 2) else c > k

    def piece(q):
        return pl.ds(pl.multiple_of(q * step, step), step)

    def col_copy(k, slot, q, way, target):
        view = colb.at[k, slot] if q is None else colb.at[k, slot, piece(q)]
        return pltpu.make_async_remote_copy(
            src_ref=view,
            dst_ref=view,
            send_sem=col_send.at[k, slot, way],
            recv_sem=col_recv.at[k, slot, 0 if q is None else q],
            device_id={"col": target},
            device_id_type=MESH,
        )

    def row_copy(k, slot, q, way, target):
        view = rowb.at[k, slot] if q is None else rowb.at[k, slot, piece(q)]
        return pltpu.make_async_remote_copy(
            src_ref=view,
            dst_ref=view,
            send_sem=row_send.at[k, slot, way],
            recv_sem=row_recv.at[k, slot, 0 if q is None else q],
            device_id={"row": target},
            device_id_type=MESH,
        )

    def col_ways(k):
        return [
            ((x == k) & skip, c + 2 * minor_col),
            ((x == k) & rise, c + minor_col),
            ((x == k) & fall, c - minor_col),
            ((x >= k) & (x + 1 < minor_col), c + 1),
            ((x <= k) & (x >= 1), c - 1),
        ]

    def row_ways():
        return [(r + 2 < n_row, r + 2), (r >= 0, r + 1 - 2 * core)]

    def col_forward(k, slot, q, ways=ALL):
        for way in ways:
            needed, target = col_ways(k)[way]

            @pl.when(needed)
            def _():
                col_copy(k, slot, q, way, target).start()

    def row_forward(k, slot, q):
        for way, (needed, target) in enumerate(row_ways()):

            @pl.when(needed)
            def _():
                row_copy(k, slot, q, way, target).start()

    def col_send_out(k, slot, ways=ALL):
        @pl.when((c == k) & col_wanted(k, slot))
        def _():
            @pl.loop(0, CHUNKS)
            def _(q):
                col_forward(k, slot, q, ways)

    def row_send_out(k, slot):
        @pl.when((r == k) & row_wanted(k, slot))
        def _():
            @pl.loop(0, CHUNKS)
            def _(q):
                row_forward(k, slot, q)

    trunk = jnp.minimum(x, 1)

    def col_relay_piece(slot, q):
        col_copy(trunk, slot, q, 0, 0).wait_recv()
        col_forward(trunk, slot, q)

    def col_relay(slot, also):
        @pl.when((c >= 2) & (x < 2) & also)
        def _():
            @pl.loop(0, CHUNKS)
            def _(q):
                col_relay_piece(slot, q)

    def row_relay_piece(slot, q):
        row_copy(core, slot, q, 0, 0).wait_recv()
        row_forward(core, slot, q)

    def row_relay(slot, also):
        @pl.when((r >= 2) & also)
        def _():
            @pl.loop(0, CHUNKS)
            def _(q):
                row_relay_piece(slot, q)

    def col_leaf(k, *slots, also=True):
        for slot in slots:

            @pl.when((x != k) & col_wanted(k, slot) & also)
            def _():
                @pl.loop(0, CHUNKS)
                def _(q):
                    col_copy(k, slot, q, 0, 0).wait_recv()
                    if minor_col > 2:
                        col_forward(k, slot, q, ALONG)

    def row_leaf(k, *slots, also=True):
        for slot in slots:

            @pl.when((core != k) & row_wanted(k, slot) & also)
            def _():
                @pl.loop(0, CHUNKS)
                def _(q):
                    row_copy(k, slot, q, 0, 0).wait_recv()

    def swap_halves():
        return pltpu.make_async_remote_copy(
            src_ref=up.at[:, mine],
            dst_ref=up.at[:, mine],
            send_sem=swap_sem.at[0],
            recv_sem=swap_sem.at[1],
            device_id={"row": r + 1 - 2 * core},
            device_id_type=MESH,
        )

    def up_copy(k, source):
        return pltpu.make_async_remote_copy(
            src_ref=upper.at[k, :, mine],
            dst_ref=up.at[pl.ds(pl.multiple_of(source * up_rows, up_rows), up_rows), mine],
            send_sem=inv_send.at[0, k],
            recv_sem=up_recv.at[source],
            device_id={"col": k},
            device_id_type=MESH,
        )

    def low_copy(k, source):
        return pltpu.make_async_remote_copy(
            src_ref=lower.at[k],
            dst_ref=low.at[pl.ds(pl.multiple_of(source * low_rows, low_rows), low_rows)],
            send_sem=inv_send.at[1, k],
            recv_sem=low_recv.at[source],
            device_id={"row": k},
            device_id_type=MESH,
        )

    def lend_left():
        return pltpu.make_async_remote_copy(
            src_ref=ul.at[0, 0],
            dst_ref=colb.at[0, 0],
            send_sem=extra_sem.at[0],
            recv_sem=extra_sem.at[1],
            device_id={"col": 0},
            device_id_type=MESH,
        )

    def pass_mixed():
        return pltpu.make_async_remote_copy(
            src_ref=mix,
            dst_ref=mix,
            send_sem=extra_sem.at[2],
            recv_sem=extra_sem.at[3],
            device_id={"col": 1},
            device_id_type=MESH,
        )

    U, Y = 0, 1

    def take_left(a, b):
        fetch_left[a][b].wait()
        ul[a, b] = ul[a, b] * keep(a, b)

    def take_right(a, b):
        fetch_right[a][b].wait()
        out[a, b] = out[a, b] * keep(a, b)

    for a in range(2):
        take_left(a, 0)
        for k in range(2):
            slot = col_slot(U, k, a)

            @pl.when((c == k) & col_wanted(k, slot))
            def _():
                colb[k, slot] = ul[a, 0]

    for b in range(2):
        take_right(0, b)

        @pl.when(r == 0)
        def _():
            rowb[0, row_slot(Y, 0, b)] = out[0, b]

    pl.semaphore_wait(barrier, greeted)

    def give_up(k):
        @pl.when((c != k) & up_has(c))
        def _():
            up_copy(k, c).start()

    give_up(0)
    for k in range(2):

        @pl.when(r != k)
        def _():
            low_copy(k, r).start()

    def core_of(panel, a, b):
        return matmul_tn(
            colb[panel, col_slot(Y, panel, a)], rowb[panel, row_slot(U, panel, b)]
        ).astype(jnp.bfloat16)

    def meet_of(panel, a, b):
        return matmul_tn(ul[a, b], colb[panel, col_slot(U, panel, a)]).astype(jnp.bfloat16)

    def subtract(panel, a, b, mixed):
        change = matmul_nt(rowb[panel, row_slot(Y, panel, b)], mixed)
        out[a, b] = (out[a, b].astype(jnp.float32) - change).astype(jnp.bfloat16)

    def update(panel, a, b, also=True):
        @pl.when((True if a > 0 else r > panel) & also)
        def _():
            mixed = matmul(meet_of(panel, a, b), core_of(panel, a, b)).astype(jnp.bfloat16)
            subtract(panel, a, b, mixed)

    def meet(panel, a, b):
        part[panel, a, b] = meet_of(panel, a, b)

    def blend(panel, a, b):
        part[panel, a, b] = matmul(part[panel, a, b], core_of(panel, a, b)).astype(jnp.bfloat16)

    def apply(panel, a, b):
        subtract(panel, a, b, part[panel, a, b])

    def wait_low(k):
        own_low(k).wait()
        for s in range(n_row):
            if s != k:
                low_copy(k, s).wait_recv()

    def solve_row(k, b, source=None):
        slot = row_slot(U, k, b)
        rowb[k, slot] = matmul(low[...], ul[0, b] if source is None else source[...]).astype(jnp.bfloat16)

    def solve_col(k, a):
        colb[k, col_slot(Y, k, a)] = matmul(up[...], out[a, 0]).astype(jnp.bfloat16)

    def share_row(b):
        rowb[1, row_slot(Y, 1, b)] = out[0, b]
        row_send_out(1, row_slot(Y, 1, b))

    even, odd = (r >= 2) & (core == 0), (r >= 2) & (core == 1)

    @pl.when(r == 0)
    def _():
        row_send_out(0, 0)
        row_send_out(0, 1)

    @pl.when(c < 2)
    def _():
        @pl.when((c == 1) & (r == 0))
        def _():
            lend_left().start()

        col_send_out(0, 0)
        col_send_out(1, 1, ALONG)
        col_send_out(1, 0, UP)
        col_send_out(1, 1, UP)
        col_send_out(1, 0, ALONG)

    for t in range(2):
        take_left(t, 1)
    for t in range(2):
        take_right(1, t)

    @pl.when(c < 2)
    def _():
        @pl.when(r == 0)
        def _():
            wait_low(0)

            @pl.when(c == 0)
            def _():
                lend_left().wait_recv()
                solve_row(0, 0, colb.at[0, 0])

            @pl.when(c != 0)
            def _():
                solve_row(0, 0)

            row_send_out(0, 2)
            solve_row(0, 1)
            row_send_out(0, 3)

        give_up(1)
        for k in range(2):

            @pl.when((c == k) & up_has(k))
            def _():
                own_up(k).wait()

        for s in range(n_col):

            @pl.when((s != c) & up_has(s))
            def _():
                up_copy(0, s).wait_recv()

        swap_halves().start()
        swap_halves().wait_recv()

        @pl.when(c == 0)
        def _():
            @pl.when(r > 0)
            def _():
                solve_col(0, 0)

            col_send_out(0, 1)
            col_send_out(0, 2, UP)
            solve_col(0, 1)
            col_send_out(0, 3, UP)

        @pl.when(r == 1)
        def _():
            wait_low(1)
            solve_row(1, 1)
            row_send_out(1, 1)

        row_relay(0, even & (c == 1))
        row_relay(1, even)
        row_relay(2, even)
        row_leaf(0, 0, 2)

        @pl.when(c == 0)
        def _():
            col_leaf(1, 1)
            crossed = matmul_tn(colb[1, col_slot(U, 1, 1)], ul[1, 0]).astype(jnp.bfloat16)
            mix[...] = matmul(crossed, core_of(0, 1, 0)).astype(jnp.bfloat16)
            pass_mixed().start()
            col_send_out(0, 2, ALONG)
            col_send_out(0, 3, ALONG)

        @pl.when(c == 1)
        def _():
            col_leaf(0, 0, 1)
            update(0, 0, 0)

            @pl.when(r > 1)
            def _():
                solve_col(1, 0)

            col_send_out(1, 2)

        row_relay(3, even)
        row_leaf(0, 1, 3)
        update(0, 0, 1, also=r == 1)

        @pl.when(r == 1)
        def _():
            share_row(1)

        @pl.when(c == 1)
        def _():
            pass_mixed().wait_recv()
            subtract(0, 1, 0, mix[...])
            solve_col(1, 1)
            col_send_out(1, 3)

        row_relay(1, odd)
        update(0, 0, 1, also=r != 1)
        col_leaf(0, 2, 3)
        update(0, 1, 1)
        row_relay(3, odd)
        row_leaf(1, 1, 3)
        col_leaf(1, 0)
        col_leaf(1, 2)
        update(1, 0, 1)
        col_leaf(1, 3)
        update(1, 1, 1)
        for panel in range(2):
            for a in range(2):

                @pl.when((c == panel) & (True if a > 0 else r > panel))
                def _():
                    out[a, 0] = colb[panel, col_slot(Y, panel, a)]

    @pl.when((c >= 2) & (r < 2))
    def _():
        give_up(1)

        @pl.when(r == 0)
        def _():
            wait_low(0)
            for b in range(2):
                solve_row(0, b)
                row_send_out(0, 2 + b)

        col_relay(0, (r == 1) & (x == 0))
        col_relay(1, x == 1)
        col_relay(2, (r == 0) & (x == 0))

        @pl.when(r == 1)
        def _():
            wait_low(1)
            for b in range(2):
                solve_row(1, b)
                row_send_out(1, b)

            col_relay(1, x == 0)
            col_leaf(0, 0, 1)
            for b in range(2):
                row_leaf(0, b, 2 + b)
                update(0, 0, b)
                share_row(b)

            col_relay(2, x == 0)

        col_relay(3, r >= 0)
        col_leaf(0, 2)
        col_leaf(1, 1)
        for panel in range(2):
            for b in range(2):
                meet(panel, 1, b)
        col_leaf(0, 3)
        for b in range(2):
            blend(0, 1, b)
            apply(0, 1, b)
        row_leaf(1, 0, 1, 2, 3)
        col_leaf(1, 3)
        for b in range(2):
            blend(1, 1, b)
            apply(1, 1, b)

    @pl.when((c >= 2) & (r >= 2))
    def _():
        main = x < 2

        def pump(slot, even_rows, odd_rows, begin=0, end=CHUNKS):
            @pl.loop(begin, end)
            def _(q):
                @pl.when(main)
                def _():
                    col_relay_piece(slot, q)

                for role, rows in ((core == 0, even_rows), (core == 1, odd_rows)):
                    for first, rate in rows:
                        for extra in range(rate):

                            @pl.when(role)
                            def _():
                                m = first * CHUNKS + q * rate + extra
                                row_relay_piece(m // CHUNKS, lax.rem(m, CHUNKS))

        give_up(1)
        pump(0, [(0, 1)], [])
        def pump_beside(slot, even_rows, odd_rows, jobs):
            for q in range(CHUNKS):
                pump(slot, even_rows, odd_rows, q, q + 1)
                if q < len(jobs) and jobs[q] is not None:
                    jobs[q]()

        def last_meet():
            col_leaf(0, 2)
            meet(0, 1, 0)

        def next_blend():
            col_leaf(1, 2)
            row_leaf(1, 0)
            blend(1, 0, 0)

        def last_blend():
            row_leaf(1, 1)
            blend(1, 0, 1)

        pump(1, [(1, 2)], [])
        col_leaf(0, 0, 1)
        row_leaf(0, 0, 2)
        col_leaf(1, 0, 1)
        at = functools.partial
        pump_beside(
            2,
            [(3, 1)],
            [(0, 2)],
            [
                at(meet, 0, 0, 0),
                at(blend, 0, 0, 0),
                at(apply, 0, 0, 0),
                at(meet, 0, 0, 1),
                at(meet, 1, 0, 0),
                at(meet, 1, 0, 1),
                at(meet, 1, 1, 0),
                at(meet, 1, 1, 1),
            ],
        )
        row_leaf(0, 1, 3)
        pump_beside(
            3,
            [],
            [],
            [
                at(blend, 0, 0, 1),
                at(apply, 0, 0, 1),
                None,
                last_meet,
                at(meet, 0, 1, 1),
                None,
                next_blend,
                last_blend,
            ],
        )
        for b in range(2):
            row_relay(2 + b, core == 1)
            row_leaf(1, 2 + b)
            apply(1, 0, b)
        col_leaf(0, 3)
        for b in range(2):
            blend(0, 1, b)
            apply(0, 1, b)
        col_leaf(1, 3)
        for b in range(2):
            blend(1, 1, b)
            apply(1, 1, b)

    for k in range(2):

        @pl.when((c != k) & up_has(c))
        def _():
            up_copy(k, c).wait_send()

        @pl.when(r != k)
        def _():
            low_copy(k, r).wait_send()

    @pl.when(c < 2)
    def _():
        swap_halves().wait_send()

        @pl.when((c == 1) & (r == 0))
        def _():
            lend_left().wait_send()

        @pl.when(c == 0)
        def _():
            pass_mixed().wait_send()

    for k in range(2):
        for slot in range(4):
            for way, (needed, target) in enumerate(col_ways(k)):

                @pl.when(needed & col_wanted(k, slot))
                def _():
                    col_copy(k, slot, None, way, target).wait_send()

            for way, (needed, target) in enumerate(row_ways()):

                @pl.when((core == k) & needed & row_wanted(k, slot))
                def _():
                    row_copy(k, slot, None, way, target).wait_send()


def body(left, right, lower_inverse, upper_inverse, ranks):
    n_row, n_col = lax.axis_size("row"), lax.axis_size("col")
    minor_col = 4 if n_col % 4 == 0 and n_col > 8 else 2
    order, width = left.shape[2:]
    upper = jnp.swapaxes(upper_inverse, 1, 2)
    tile = (order, width)
    vmem = pl.BlockSpec(memory_space=pltpu.VMEM)
    hbm = pl.BlockSpec(memory_space=pltpu.HBM)
    return pl.pallas_call(
        functools.partial(kernel, n_row, n_col, minor_col),
        out_shape=pltpu.VMEM(right.shape, jnp.bfloat16),
        in_specs=[pl.BlockSpec(memory_space=pltpu.SMEM)] + [hbm] * 4,
        out_specs=vmem,
        scratch_shapes=[
            pltpu.VMEM((2, 2) + tile, jnp.bfloat16),
            pltpu.VMEM((2, 4) + tile, jnp.bfloat16),
            pltpu.VMEM((2, 4) + tile, jnp.bfloat16),
            pltpu.VMEM((order, order), jnp.bfloat16),
            pltpu.VMEM((order, order), jnp.bfloat16),
            pltpu.VMEM((width, width), jnp.bfloat16),
            pltpu.VMEM((2, 2, 2, width, width), jnp.bfloat16),
            pltpu.SemaphoreType.DMA((2, 4, 5)),
            pltpu.SemaphoreType.DMA((2, 4, CHUNKS)),
            pltpu.SemaphoreType.DMA((2, 4, 2)),
            pltpu.SemaphoreType.DMA((2, 4, CHUNKS)),
            pltpu.SemaphoreType.DMA((2, 2)),
            pltpu.SemaphoreType.DMA((n_row,)),
            pltpu.SemaphoreType.DMA((n_col,)),
            pltpu.SemaphoreType.DMA((2, 2, 2)),
            pltpu.SemaphoreType.DMA((2,)),
            pltpu.SemaphoreType.DMA((4,)),
        ],
        compiler_params=pltpu.CompilerParams(
            collective_id=0, has_side_effects=True, vmem_limit_bytes=60 * 1024 * 1024
        ),
        cost_estimate=pl.CostEstimate(
            flops=2_000_000_000, bytes_accessed=4_000_000, transcendentals=0
        ),
    )(ranks, left, right, lower_inverse, upper)


def solution(mesh):
    placed = (
        P("row", "col", None, None),
        P("row", "col", None, None),
        P(None, "row", None),
        P(None, None, "col"),
        P("row", "col"),
    )
    return jax.shard_map(
        body, mesh=mesh, in_specs=placed, out_specs=P("row", "col", None, None), check_vma=False
    )
```

```python
import functools

import jax
import jax.numpy as jnp
from jax import lax
from jax.experimental import pallas as pl
from jax.experimental.pallas import tpu as pltpu
from jax.sharding import PartitionSpec as P

CHUNKS = 8
MESH = pl.DeviceIdType.MESH
UP, ALONG = (0, 1, 2), (3, 4)
ALL = UP + ALONG


def matmul(a, b):
    return jnp.dot(a, b, preferred_element_type=jnp.float32)


def matmul_tn(a, b):
    return lax.dot_general(a, b, (((0,), (0,)), ((), ())), preferred_element_type=jnp.float32)


def matmul_nt(a, b):
    return lax.dot_general(a, b, (((1,), (1,)), ((), ())), preferred_element_type=jnp.float32)


def kernel(
    n_row, n_col, minor_col, ranks, left, right, lower, upper, out,
    ul, colb, rowb, low, up, mix, part,
    col_send, col_recv, row_send, row_recv, inv_send, low_recv, up_recv, fetch_sem, swap_sem, extra_sem,
):
    r, c = lax.axis_index("row"), lax.axis_index("col")
    x, core = lax.rem(c, minor_col), lax.rem(r, 2)
    order, width = left.shape[2], left.shape[3]
    step = order // CHUNKS
    fetch_left = [
        [pltpu.make_async_copy(left.at[a, b], ul.at[a, b], fetch_sem.at[0, a, b]) for b in range(2)]
        for a in range(2)
    ]
    fetch_right = [
        [pltpu.make_async_copy(right.at[a, b], out.at[a, b], fetch_sem.at[1, a, b]) for b in range(2)]
        for a in range(2)
    ]
    @pl.when(c < 2)
    def _():
        up[...] = jnp.zeros_like(up)

    barrier = pltpu.get_barrier_semaphore()

    def greet(needed, **target):
        @pl.when(needed)
        def _():
            pl.semaphore_signal(barrier, inc=1, device_id=target, device_id_type=MESH)

    def count(*needed):
        return sum(flag.astype(jnp.int32) for flag in needed)

    for d in range(n_col - 1, 0, -1):
        greet(c < 2, col=lax.rem(c + d, n_col))
    for d in range(1, n_row):
        greet(r < 2, row=lax.rem(r + d, n_row))
    depth = n_col // minor_col
    z = lax.div(c, minor_col)
    even_z = lax.rem(z, 2) == 0
    if depth > 2:
        skip, rise, fall = even_z & (z + 2 < depth), even_z & (z >= 2) & (z + 1 < depth), z == 2
        greet(even_z & (z >= 2), col=c - 2 * minor_col)
        greet(jnp.logical_not(even_z) & (z >= 3), col=c - minor_col)
        greet(z == 1, col=c + minor_col)
    else:
        skip, rise, fall = z < 0, z + 1 < depth, z < 0
        greet(z >= 1, col=c - minor_col)
    greet(r >= 2, row=r - 2)
    greet(r >= 0, row=r + 1 - 2 * core)
    greet(x + 1 < minor_col, col=c + 1)
    greet(x >= 1, col=c - 1)
    greeted = 1 + count(
        r + 2 < n_row, x + 1 < minor_col, x >= 1, skip, rise, fall, r != 0, r != 1, c != 0, c != 1
    )

    for a in range(2):
        fetch_left[a][0].start()
    for b in range(2):
        fetch_right[0][b].start()
    for a in range(2):
        fetch_left[a][1].start()
    for b in range(2):
        fetch_right[1][b].start()

    half = order // 2
    mine = pl.ds(pl.multiple_of(core * half, half), half)
    up_rows, low_rows = upper.shape[1], lower.shape[1]

    def own_up(k):
        return pltpu.make_async_copy(
            upper.at[k, :, mine], up.at[pl.ds(k * up_rows, up_rows), mine], inv_send.at[0, k]
        )

    def own_low(k):
        return pltpu.make_async_copy(
            lower.at[k], low.at[pl.ds(k * low_rows, low_rows)], inv_send.at[1, k]
        )

    def up_has(source):
        return (source + 1) * up_rows > core * half

    for k in range(2):

        @pl.when((c == k) & up_has(k))
        def _():
            own_up(k).start()

        @pl.when(r == k)
        def _():
            own_low(k).start()

    lanes = lax.broadcasted_iota(jnp.int32, (1, width), 1)

    def keep(a, b):
        return (lanes < ranks[a, b]).astype(jnp.float32).astype(jnp.bfloat16)

    def col_slot(kind, k, t):
        return 2 * t + kind if k == 0 else 2 * kind + t

    def row_slot(kind, k, t):
        return 2 * (1 - kind) + t if k == 0 else 2 * kind + t

    def col_wanted(k, slot):
        t = slot // 2 if k == 0 else slot % 2
        return True if t > 0 else r > k

    def row_wanted(k, slot):
        return True if slot % 2 > 0 or (k, slot) == (0, 2) else c > k

    def piece(q):
        return pl.ds(pl.multiple_of(q * step, step), step)

    def col_copy(k, slot, q, way, target):
        view = colb.at[k, slot] if q is None else colb.at[k, slot, piece(q)]
        return pltpu.make_async_remote_copy(
            src_ref=view,
            dst_ref=view,
            send_sem=col_send.at[k, slot, way],
            recv_sem=col_recv.at[k, slot, 0 if q is None else q],
            device_id={"col": target},
            device_id_type=MESH,
        )

    def row_copy(k, slot, q, way, target):
        view = rowb.at[k, slot] if q is None else rowb.at[k, slot, piece(q)]
        return pltpu.make_async_remote_copy(
            src_ref=view,
            dst_ref=view,
            send_sem=row_send.at[k, slot, way],
            recv_sem=row_recv.at[k, slot, 0 if q is None else q],
            device_id={"row": target},
            device_id_type=MESH,
        )

    def col_ways(k):
        return [
            ((x == k) & skip, c + 2 * minor_col),
            ((x == k) & rise, c + minor_col),
            ((x == k) & fall, c - minor_col),
            ((x >= k) & (x + 1 < minor_col), c + 1),
            ((x <= k) & (x >= 1), c - 1),
        ]

    def row_ways():
        return [(r + 2 < n_row, r + 2), (r >= 0, r + 1 - 2 * core)]

    def col_forward(k, slot, q, ways=ALL):
        for way in ways:
            needed, target = col_ways(k)[way]

            @pl.when(needed)
            def _():
                col_copy(k, slot, q, way, target).start()

    def row_forward(k, slot, q):
        for way, (needed, target) in enumerate(row_ways()):

            @pl.when(needed)
            def _():
                row_copy(k, slot, q, way, target).start()

    def col_send_out(k, slot, ways=ALL):
        @pl.when((c == k) & col_wanted(k, slot))
        def _():
            @pl.loop(0, CHUNKS)
            def _(q):
                col_forward(k, slot, q, ways)

    def row_send_out(k, slot):
        @pl.when((r == k) & row_wanted(k, slot))
        def _():
            @pl.loop(0, CHUNKS)
            def _(q):
                row_forward(k, slot, q)

    trunk = jnp.minimum(x, 1)

    def col_relay_piece(slot, q):
        col_copy(trunk, slot, q, 0, 0).wait_recv()
        col_forward(trunk, slot, q)

    def col_relay(slot, also):
        @pl.when((c >= 2) & (x < 2) & also)
        def _():
            @pl.loop(0, CHUNKS)
            def _(q):
                col_relay_piece(slot, q)

    def row_relay_piece(slot, q):
        row_copy(core, slot, q, 0, 0).wait_recv()
        row_forward(core, slot, q)

    def row_relay(slot, also):
        @pl.when((r >= 2) & also)
        def _():
            @pl.loop(0, CHUNKS)
            def _(q):
                row_relay_piece(slot, q)

    def col_leaf(k, *slots, also=True):
        for slot in slots:

            @pl.when((x != k) & col_wanted(k, slot) & also)
            def _():
                @pl.loop(0, CHUNKS)
                def _(q):
                    col_copy(k, slot, q, 0, 0).wait_recv()
                    if minor_col > 2:
                        col_forward(k, slot, q, ALONG)

    def row_leaf(k, *slots, also=True):
        for slot in slots:

            @pl.when((core != k) & row_wanted(k, slot) & also)
            def _():
                @pl.loop(0, CHUNKS)
                def _(q):
                    row_copy(k, slot, q, 0, 0).wait_recv()

    def swap_halves():
        return pltpu.make_async_remote_copy(
            src_ref=up.at[:, mine],
            dst_ref=up.at[:, mine],
            send_sem=swap_sem.at[0],
            recv_sem=swap_sem.at[1],
            device_id={"row": r + 1 - 2 * core},
            device_id_type=MESH,
        )

    def up_copy(k, source):
        return pltpu.make_async_remote_copy(
            src_ref=upper.at[k, :, mine],
            dst_ref=up.at[pl.ds(pl.multiple_of(source * up_rows, up_rows), up_rows), mine],
            send_sem=inv_send.at[0, k],
            recv_sem=up_recv.at[source],
            device_id={"col": k},
            device_id_type=MESH,
        )

    def low_copy(k, source):
        return pltpu.make_async_remote_copy(
            src_ref=lower.at[k],
            dst_ref=low.at[pl.ds(pl.multiple_of(source * low_rows, low_rows), low_rows)],
            send_sem=inv_send.at[1, k],
            recv_sem=low_recv.at[source],
            device_id={"row": k},
            device_id_type=MESH,
        )

    def lend_left():
        return pltpu.make_async_remote_copy(
            src_ref=ul.at[0, 0],
            dst_ref=colb.at[0, 0],
            send_sem=extra_sem.at[0],
            recv_sem=extra_sem.at[1],
            device_id={"col": 0},
            device_id_type=MESH,
        )

    def pass_mixed():
        return pltpu.make_async_remote_copy(
            src_ref=mix,
            dst_ref=mix,
            send_sem=extra_sem.at[2],
            recv_sem=extra_sem.at[3],
            device_id={"col": 1},
            device_id_type=MESH,
        )

    U, Y = 0, 1

    def take_left(a, b):
        fetch_left[a][b].wait()
        ul[a, b] = ul[a, b] * keep(a, b)

    def take_right(a, b):
        fetch_right[a][b].wait()
        out[a, b] = out[a, b] * keep(a, b)

    for a in range(2):
        take_left(a, 0)
        for k in range(2):
            slot = col_slot(U, k, a)

            @pl.when((c == k) & col_wanted(k, slot))
            def _():
                colb[k, slot] = ul[a, 0]

    for b in range(2):
        take_right(0, b)

        @pl.when(r == 0)
        def _():
            rowb[0, row_slot(Y, 0, b)] = out[0, b]

    pl.semaphore_wait(barrier, greeted)

    def give_up(k):
        @pl.when((c != k) & up_has(c))
        def _():
            up_copy(k, c).start()

    give_up(0)
    for k in range(2):

        @pl.when(r != k)
        def _():
            low_copy(k, r).start()

    def core_of(panel, a, b):
        return matmul_tn(
            colb[panel, col_slot(Y, panel, a)], rowb[panel, row_slot(U, panel, b)]
        ).astype(jnp.bfloat16)

    def meet_of(panel, a, b):
        return matmul_tn(ul[a, b], colb[panel, col_slot(U, panel, a)]).astype(jnp.bfloat16)

    def subtract(panel, a, b, mixed):
        change = matmul_nt(rowb[panel, row_slot(Y, panel, b)], mixed)
        out[a, b] = (out[a, b].astype(jnp.float32) - change).astype(jnp.bfloat16)

    def update(panel, a, b, also=True):
        @pl.when((True if a > 0 else r > panel) & also)
        def _():
            mixed = matmul(meet_of(panel, a, b), core_of(panel, a, b)).astype(jnp.bfloat16)
            subtract(panel, a, b, mixed)

    def meet(panel, a, b):
        part[panel, a, b] = meet_of(panel, a, b)

    def blend(panel, a, b):
        part[panel, a, b] = matmul(part[panel, a, b], core_of(panel, a, b)).astype(jnp.bfloat16)

    def finish(panel, a):
        mixed = [
            matmul(part[panel, a, b], core_of(panel, a, b)).astype(jnp.bfloat16) for b in range(2)
        ]
        for b in range(2):
            subtract(panel, a, b, mixed[b])

    def apply(panel, a, b):
        subtract(panel, a, b, part[panel, a, b])

    def wait_low(k):
        own_low(k).wait()
        for s in range(n_row):
            if s != k:
                low_copy(k, s).wait_recv()

    def solve_row(k, b, source=None):
        slot = row_slot(U, k, b)
        rowb[k, slot] = matmul(low[...], ul[0, b] if source is None else source[...]).astype(jnp.bfloat16)

    def solve_col(k, a):
        colb[k, col_slot(Y, k, a)] = matmul(up[...], out[a, 0]).astype(jnp.bfloat16)

    def share_row(b):
        rowb[1, row_slot(Y, 1, b)] = out[0, b]
        row_send_out(1, row_slot(Y, 1, b))

    even, odd = (r >= 2) & (core == 0), (r >= 2) & (core == 1)

    @pl.when(r == 0)
    def _():
        row_send_out(0, 0)
        row_send_out(0, 1)

    @pl.when(c < 2)
    def _():
        @pl.when((c == 1) & (r == 0))
        def _():
            lend_left().start()

        col_send_out(0, 0)
        col_send_out(1, 1, ALONG)
        col_send_out(1, 0, UP)
        col_send_out(1, 1, UP)
        col_send_out(1, 0, ALONG)

    for t in range(2):
        take_left(t, 1)
    for t in range(2):
        take_right(1, t)

    @pl.when(c < 2)
    def _():
        @pl.when(r == 0)
        def _():
            wait_low(0)

            @pl.when(c == 0)
            def _():
                lend_left().wait_recv()
                solve_row(0, 0, colb.at[0, 0])

            @pl.when(c != 0)
            def _():
                solve_row(0, 0)

            row_send_out(0, 2)
            solve_row(0, 1)
            row_send_out(0, 3)

        give_up(1)
        for k in range(2):

            @pl.when((c == k) & up_has(k))
            def _():
                own_up(k).wait()

        for s in range(n_col):

            @pl.when((s != c) & up_has(s))
            def _():
                up_copy(0, s).wait_recv()

        swap_halves().start()
        swap_halves().wait_recv()

        @pl.when(c == 0)
        def _():
            @pl.when(r > 0)
            def _():
                solve_col(0, 0)

            col_send_out(0, 1)
            col_send_out(0, 2, UP)
            solve_col(0, 1)
            col_send_out(0, 3, UP)

        @pl.when(r == 1)
        def _():
            wait_low(1)
            solve_row(1, 1)
            row_send_out(1, 1)

        row_relay(0, even & (c == 1))
        row_relay(1, even)
        row_relay(2, even)
        row_leaf(0, 0, 2)

        @pl.when(c == 0)
        def _():
            col_leaf(1, 1)
            crossed = matmul_tn(colb[1, col_slot(U, 1, 1)], ul[1, 0]).astype(jnp.bfloat16)
            mix[...] = matmul(crossed, core_of(0, 1, 0)).astype(jnp.bfloat16)
            pass_mixed().start()
            col_send_out(0, 2, ALONG)
            col_send_out(0, 3, ALONG)

        @pl.when(c == 1)
        def _():
            col_leaf(0, 0, 1)
            update(0, 0, 0)

            @pl.when(r > 1)
            def _():
                solve_col(1, 0)

            col_send_out(1, 2)

        row_relay(3, even)
        row_leaf(0, 1, 3)
        update(0, 0, 1, also=r == 1)

        @pl.when(r == 1)
        def _():
            share_row(1)

        @pl.when(c == 1)
        def _():
            pass_mixed().wait_recv()
            subtract(0, 1, 0, mix[...])
            solve_col(1, 1)
            col_send_out(1, 3)

        row_relay(1, odd)
        update(0, 0, 1, also=r != 1)
        col_leaf(0, 2, 3)
        update(0, 1, 1)
        row_relay(3, odd)
        row_leaf(1, 1, 3)
        col_leaf(1, 0)
        col_leaf(1, 2)
        update(1, 0, 1)
        col_leaf(1, 3)
        update(1, 1, 1)
        for panel in range(2):
            for a in range(2):

                @pl.when((c == panel) & (True if a > 0 else r > panel))
                def _():
                    out[a, 0] = colb[panel, col_slot(Y, panel, a)]

    @pl.when((c >= 2) & (r < 2))
    def _():
        give_up(1)

        @pl.when(r == 0)
        def _():
            wait_low(0)
            for b in range(2):
                solve_row(0, b)
                row_send_out(0, 2 + b)

        col_relay(0, (r == 1) & (x == 0))
        col_relay(1, x == 1)
        col_relay(2, (r == 0) & (x == 0))

        @pl.when(r == 1)
        def _():
            wait_low(1)
            for b in range(2):
                solve_row(1, b)
                row_send_out(1, b)

            col_relay(1, x == 0)
            col_leaf(0, 0, 1)
            for b in range(2):
                row_leaf(0, b, 2 + b)
                update(0, 0, b)
                share_row(b)

            col_relay(2, x == 0)

        col_relay(3, r >= 0)
        col_leaf(0, 2)
        col_leaf(1, 1)
        for panel in range(2):
            for b in range(2):
                meet(panel, 1, b)
        col_leaf(0, 3)
        finish(0, 1)
        row_leaf(1, 0, 1, 2, 3)
        col_leaf(1, 3)
        finish(1, 1)

    @pl.when((c >= 2) & (r >= 2))
    def _():
        main = x < 2

        def pump(slot, even_rows, odd_rows, begin=0, end=CHUNKS):
            @pl.loop(begin, end)
            def _(q):
                @pl.when(main)
                def _():
                    col_relay_piece(slot, q)

                for role, rows in ((core == 0, even_rows), (core == 1, odd_rows)):
                    for first, rate in rows:
                        for extra in range(rate):

                            @pl.when(role)
                            def _():
                                m = first * CHUNKS + q * rate + extra
                                row_relay_piece(m // CHUNKS, lax.rem(m, CHUNKS))

        give_up(1)
        pump(0, [(0, 1)], [])
        def pump_beside(slot, even_rows, odd_rows, jobs):
            for q in range(CHUNKS):
                pump(slot, even_rows, odd_rows, q, q + 1)
                if q < len(jobs) and jobs[q] is not None:
                    jobs[q]()

        def last_meet():
            col_leaf(0, 2)
            meet(0, 1, 0)

        def next_blend():
            col_leaf(1, 2)
            row_leaf(1, 0)
            blend(1, 0, 0)

        def last_blend():
            row_leaf(1, 1)
            blend(1, 0, 1)

        pump(1, [(1, 2)], [])
        col_leaf(0, 0, 1)
        row_leaf(0, 0, 2)
        col_leaf(1, 0, 1)
        at = functools.partial
        pump_beside(
            2,
            [(3, 1)],
            [(0, 2)],
            [
                at(meet, 0, 0, 0),
                at(blend, 0, 0, 0),
                at(apply, 0, 0, 0),
                at(meet, 0, 0, 1),
                at(meet, 1, 0, 0),
                at(meet, 1, 0, 1),
                at(meet, 1, 1, 0),
                at(meet, 1, 1, 1),
            ],
        )
        row_leaf(0, 1, 3)
        pump_beside(
            3,
            [],
            [],
            [
                at(blend, 0, 0, 1),
                at(apply, 0, 0, 1),
                None,
                last_meet,
                at(meet, 0, 1, 1),
                None,
                next_blend,
                last_blend,
            ],
        )
        for b in range(2):
            row_relay(2 + b, core == 1)
        row_leaf(1, 2, 3)
        for b in range(2):
            apply(1, 0, b)
        col_leaf(0, 3)
        finish(0, 1)
        col_leaf(1, 3)
        finish(1, 1)

    for k in range(2):

        @pl.when((c != k) & up_has(c))
        def _():
            up_copy(k, c).wait_send()

        @pl.when(r != k)
        def _():
            low_copy(k, r).wait_send()

    @pl.when(c < 2)
    def _():
        swap_halves().wait_send()

        @pl.when((c == 1) & (r == 0))
        def _():
            lend_left().wait_send()

        @pl.when(c == 0)
        def _():
            pass_mixed().wait_send()

    for k in range(2):
        for slot in range(4):
            for way, (needed, target) in enumerate(col_ways(k)):

                @pl.when(needed & col_wanted(k, slot))
                def _():
                    col_copy(k, slot, None, way, target).wait_send()

            for way, (needed, target) in enumerate(row_ways()):

                @pl.when((core == k) & needed & row_wanted(k, slot))
                def _():
                    row_copy(k, slot, None, way, target).wait_send()


def body(left, right, lower_inverse, upper_inverse, ranks):
    n_row, n_col = lax.axis_size("row"), lax.axis_size("col")
    minor_col = 4 if n_col % 4 == 0 and n_col > 8 else 2
    order, width = left.shape[2:]
    upper = jnp.swapaxes(upper_inverse, 1, 2)
    tile = (order, width)
    vmem = pl.BlockSpec(memory_space=pltpu.VMEM)
    hbm = pl.BlockSpec(memory_space=pltpu.HBM)
    return pl.pallas_call(
        functools.partial(kernel, n_row, n_col, minor_col),
        out_shape=pltpu.VMEM(right.shape, jnp.bfloat16),
        in_specs=[pl.BlockSpec(memory_space=pltpu.SMEM)] + [hbm] * 4,
        out_specs=vmem,
        scratch_shapes=[
            pltpu.VMEM((2, 2) + tile, jnp.bfloat16),
            pltpu.VMEM((2, 4) + tile, jnp.bfloat16),
            pltpu.VMEM((2, 4) + tile, jnp.bfloat16),
            pltpu.VMEM((order, order), jnp.bfloat16),
            pltpu.VMEM((order, order), jnp.bfloat16),
            pltpu.VMEM((width, width), jnp.bfloat16),
            pltpu.VMEM((2, 2, 2, width, width), jnp.bfloat16),
            pltpu.SemaphoreType.DMA((2, 4, 5)),
            pltpu.SemaphoreType.DMA((2, 4, CHUNKS)),
            pltpu.SemaphoreType.DMA((2, 4, 2)),
            pltpu.SemaphoreType.DMA((2, 4, CHUNKS)),
            pltpu.SemaphoreType.DMA((2, 2)),
            pltpu.SemaphoreType.DMA((n_row,)),
            pltpu.SemaphoreType.DMA((n_col,)),
            pltpu.SemaphoreType.DMA((2, 2, 2)),
            pltpu.SemaphoreType.DMA((2,)),
            pltpu.SemaphoreType.DMA((4,)),
        ],
        compiler_params=pltpu.CompilerParams(
            collective_id=0, has_side_effects=True, vmem_limit_bytes=60 * 1024 * 1024
        ),
        cost_estimate=pl.CostEstimate(
            flops=2_000_000_000, bytes_accessed=4_000_000, transcendentals=0
        ),
    )(ranks, left, right, lower_inverse, upper)


def solution(mesh):
    placed = (
        P("row", "col", None, None),
        P("row", "col", None, None),
        P(None, "row", None),
        P(None, None, "col"),
        P("row", "col"),
    )
    return jax.shard_map(
        body, mesh=mesh, in_specs=placed, out_specs=P("row", "col", None, None), check_vma=False
    )
```
